32 devices in a mesh: role: 4 (over y, x), dp: 2 (over core), tp: 4 (over z).
Axes of the slice: x: 2, y: 2, z: 4, core: 2. Of those that a mesh axis runs over, the one named last changes fastest.
Arguments:
- ref_logits: bfloat16 [1024, 77824], P(('role', 'dp'), 'tp'), may hold values from -30 to 250
- token_ids: int32 [1024], P(('role', 'dp')), may hold values from 0 to 77823
- old_logp: bfloat16 [1024], P(('role', 'dp')), may hold values from -28 to -4
- owner_of_row: int32 [1024], P(('role', 'dp')), may hold values from 0 to 7, as said below
- lengths: int32 [16], P(('role', 'dp')), may hold values from 1 to 64
- rewards: float32 [16], replicated, may hold values from 0 to 1
- group_ids: int32 [16], replicated, may hold values from 0 to 1
- pol_logits: bfloat16 [1536, 77824], P(('role', 'dp'), 'tp'), may hold values from -30 to 250
Outputs:
- grad_logits: bfloat16 [1536, 77824], P(('role', 'dp'), 'tp')
- token_loss: float32 [1536], P(('role', 'dp'))
The draws below stay inside these ranges and needn't reach their ends.
Inputs may be any that keep to these rules, and one draw needn't show every extreme that they name: `owner_of_row`: among the rows of one owner (aligned blocks of 128 rows) at most 24 name the same owner; one owner drawn from the seed is named by exactly 24 rows in every block.
All inputs are finite; a program needn't handle non-finite values.
Results may differ from the reference program's by a relative error of at most 0.001.
Values may be sent and summed in bfloat16 or wider, within the bound.
A program may use at most 128 MiB of HBM per device.

```python
import math
import jax
import jax.numpy as jnp
import numpy as np
from jax import lax

V = 77824
LMAX = 64
SEQ_DEV = 2
OWNERS = 8
R_DEV = 128
ROWS = 1024
SEQS = 16
NGROUP = 2
CAP = 24
PACKED = 1536


def draw_owner_of_row(key, part):
    slot_count = OWNERS * CAP
    fixed_owner = jax.random.randint(jax.random.fold_in(key, 1), (), 0, OWNERS)
    slot_owner = jnp.arange(slot_count) // CAP

    def one_block(block_key):
        key_extra = jax.random.fold_in(block_key, 3)
        key_rank = jax.random.fold_in(block_key, 4)
        key_shuffle = jax.random.fold_in(block_key, 5)
        extra_owner = jax.random.randint(key_extra, (), 0, OWNERS)
        slot_ranks = jax.random.permutation(key_rank, slot_count)
        favoured = (slot_owner == fixed_owner) | (slot_owner == extra_owner)
        scores = slot_ranks + jnp.where(favoured, -slot_count, 0)
        picked_order = jnp.argsort(scores, stable=True)
        chosen = slot_owner[picked_order[:R_DEV]]
        return chosen[jax.random.permutation(key_shuffle, R_DEV)]
    block_keys = jax.random.split(jax.random.fold_in(key, 2), OWNERS)
    return jax.vmap(one_block)(block_keys).reshape(ROWS).astype(jnp.int32)


def draw_lengths(key, part):
    seq_index = jnp.arange(SEQS)
    block_index = seq_index // SEQ_DEV
    top_len = jnp.maximum(LMAX * (OWNERS + 3 * block_index) // (4 * OWNERS), 1)
    low_len = jnp.maximum(top_len // 2, 1)
    drawn = jax.random.randint(jax.random.fold_in(key, 7), (SEQS,), low_len, top_len + 1)
    return jnp.where(seq_index == SEQS - 1, LMAX, drawn).astype(jnp.int32)


def draw_old_logp(key, part):
    values = -16.0 + 3.0 * jax.random.truncated_normal(jax.random.fold_in(key, 12), -4.0, 4.0, (ROWS,), jnp.float32)
    return values.astype(jnp.bfloat16)


def logit_table(key, row_total):
    base_draw = jax.random.truncated_normal(jax.random.fold_in(key, 31), -6.0, 6.0, (row_total, V), jnp.float32)
    values = 3.0 * base_draw
    return values.astype(jnp.bfloat16)


def draw_ref_logits(key, part):
    return logit_table(jax.random.fold_in(key, 41), ROWS)


def draw_pol_logits(key, part):
    return logit_table(jax.random.fold_in(key, 42), PACKED)


def with_ends(entries, rng, low, high):
    longest = entries.shape.index(max(entries.shape))
    spots = []
    for shift in (0, 1):
        where = [jax.random.randint(jax.random.fold_in(rng, axis), (), 0, length) for axis, length in enumerate(entries.shape)]
        where[longest] = (where[longest] + shift) % entries.shape[longest]
        spots.append(tuple(where))
    return entries.at[spots[0]].set(low).at[spots[1]].set(high)


def ranked_wide(rng, extent, amount, lean):
    weights = [min(1 << octave, amount + 1 - (1 << octave)) * (1 << 20) // math.isqrt((1 << octave) ** lean) + 1 for octave in range((amount + 1).bit_length()) if 1 << octave <= amount]
    spread = 1 + sum(weights) // (1 << 30)
    table = np.cumsum(np.array([max(1, weight // spread) for weight in weights]))
    pick = jax.random.randint(jax.random.fold_in(rng, 1), extent, 0, int(table[len(weights) - 1]))
    start = jnp.left_shift(1, jnp.searchsorted(jnp.asarray(table, jnp.int32), pick, side="right").astype(jnp.int32))
    rank = start - 1 + jax.random.randint(jax.random.fold_in(rng, 4), extent, 0, 1 << 30) % jnp.minimum(start, amount + 1 - start)
    return jax.random.permutation(jax.random.fold_in(rng, 2), amount)[rank].astype(jnp.int32)


def setup_inputs(seed: int = 0) -> dict:
    key_list = jax.random.split(jax.random.key(seed), 9)
    ref_logits = draw_ref_logits(jax.random.fold_in(key_list[8], 71), 0)
    token_ids = with_ends(ranked_wide(key_list[1], (ROWS,), V, 2), jax.random.fold_in(key_list[1], 3), 0, V - 1).astype(jnp.int32)
    old_logp = draw_old_logp(jax.random.fold_in(key_list[8], 71), 0)
    owner_of_row = draw_owner_of_row(jax.random.fold_in(key_list[8], 71), 0)
    lengths = draw_lengths(jax.random.fold_in(key_list[8], 71), 0)
    rewards = jnp.clip(jax.random.uniform(key_list[5], (SEQS,), jnp.float32, 0.0, 1.0), 0.0, 1.0)
    group_ids = with_ends(jax.random.randint(key_list[6], (SEQS,), 0, NGROUP), jax.random.fold_in(key_list[6], 1), 0, NGROUP - 1).astype(jnp.int32)
    pol_logits = draw_pol_logits(jax.random.fold_in(key_list[8], 71), 0)
    return {"ref_logits": ref_logits, "token_ids": token_ids, "old_logp": old_logp, "owner_of_row": owner_of_row, "lengths": lengths, "rewards": rewards, "group_ids": group_ids, "pol_logits": pol_logits}


kl_weight = 0.04
low_bound = 0.8
high_bound = 1.2
dual_bound = 3.0
ratio_clamp = 20.0


def block_terms(policy, ref_rows, tok_rows, old_rows, adv_rows, valid_rows, loss_scale):
    policy = policy.astype(jnp.float32)
    ref_rows = ref_rows.astype(jnp.float32)
    peak_p = jnp.max(policy, axis=1)
    policy_exp = jnp.exp(policy - peak_p[:, None])
    total_p = jnp.sum(policy_exp, axis=1)
    peak_q = jnp.max(ref_rows, axis=1)
    total_q = jnp.sum(jnp.exp(ref_rows - peak_q[:, None]), axis=1)
    cross_sum = jnp.sum(policy_exp * (policy - ref_rows), axis=1)
    token_hit = jnp.arange(V)[None, :] == tok_rows[:, None]
    token_logit = jnp.sum(jnp.where(token_hit, policy, 0.0), axis=1)
    log_p = peak_p + jnp.log(total_p)
    log_q = peak_q + jnp.log(total_q)
    mean_gap = cross_sum / total_p
    kl_term = mean_gap - log_p + log_q
    raw_log_ratio = token_logit - log_p - old_rows.astype(jnp.float32)
    prob_ratio = jnp.exp(jnp.clip(raw_log_ratio, -ratio_clamp, ratio_clamp))
    plain_loss = -adv_rows * prob_ratio
    clipped_loss = -adv_rows * jnp.clip(prob_ratio, low_bound, high_bound)
    upper_loss = jnp.maximum(plain_loss, clipped_loss)
    dual_loss = -dual_bound * adv_rows
    negative = adv_rows < 0.0
    policy_loss = jnp.where(negative, jnp.minimum(upper_loss, dual_loss), upper_loss)
    token_losses = jnp.where(valid_rows, policy_loss + kl_weight * kl_term, 0.0)
    inside = (prob_ratio > low_bound) & (prob_ratio < high_bound)
    token_coef = jnp.where((plain_loss >= clipped_loss) | inside, plain_loss, 0.0)
    token_coef = jnp.where(negative & (upper_loss > dual_loss), 0.0, token_coef)
    token_coef = jnp.where(jnp.abs(raw_log_ratio) < ratio_clamp, token_coef, 0.0)
    policy_prob = policy_exp / total_p[:, None]
    grad_rows = token_coef[:, None] * (token_hit.astype(jnp.float32) - policy_prob)
    grad_rows = grad_rows + kl_weight * policy_prob * ((policy - ref_rows) - mean_gap[:, None])
    grad_rows = jnp.where(valid_rows[:, None], loss_scale * grad_rows, 0.0).astype(jnp.bfloat16)
    return grad_rows, token_losses


def reference(ref_logits, token_ids, old_logp, owner_of_row, lengths, rewards, group_ids, pol_logits):
    member = (group_ids[:, None] == jnp.arange(NGROUP)[None, :]).astype(jnp.float32)
    group_total = jnp.sum(member * rewards[:, None], axis=0)
    group_count = jnp.sum(member, axis=0)
    group_mean = group_total / jnp.maximum(group_count, 1.0)
    advantage = rewards - jnp.sum(member * group_mean[None, :], axis=1)
    row_index = jnp.arange(ROWS)
    sequence = row_index // LMAX
    valid = (row_index % LMAX) < lengths[sequence]
    valid_total = jnp.sum(valid.astype(jnp.float32))
    loss_scale = ROWS / valid_total
    owner_block = owner_of_row.reshape(OWNERS, R_DEV)
    owner_hot = (owner_block[:, :, None] == jnp.arange(OWNERS)[None, None, :]).astype(jnp.int32)
    earlier = jnp.cumsum(owner_hot, axis=1) - owner_hot
    row_rank = jnp.sum(earlier * owner_hot, axis=2).reshape(ROWS)
    slot = (owner_of_row * (OWNERS * CAP) + (row_index // R_DEV) * CAP + row_rank).astype(jnp.int32)
    row_adv = advantage[sequence]

    def one_block(block_args):
        block_slot, ref_rows, tok_rows, old_rows, adv_rows, valid_rows = block_args
        policy = pol_logits[block_slot]
        return block_terms(policy, ref_rows, tok_rows, old_rows, adv_rows, valid_rows, loss_scale)

    grad_blocks, loss_blocks = lax.map(one_block, (slot.reshape(OWNERS, R_DEV), ref_logits.reshape(OWNERS, R_DEV, V), token_ids.reshape(OWNERS, R_DEV), old_logp.reshape(OWNERS, R_DEV), row_adv.reshape(OWNERS, R_DEV), valid.reshape(OWNERS, R_DEV)))
    grad_logits = jnp.zeros((PACKED, V), jnp.bfloat16).at[slot].set(grad_blocks.reshape(ROWS, V))
    token_loss = jnp.zeros((PACKED,), jnp.float32).at[slot].set(loss_blocks.reshape(ROWS))
    return grad_logits, token_loss
```

```python
import functools

import jax
import jax.numpy as jnp
from jax import lax
from jax.experimental import pallas as pl
from jax.experimental.pallas import tpu as pltpu
from jax.sharding import PartitionSpec as P

kl_weight = 0.04
low_bound = 0.8
high_bound = 1.2
dual_bound = 3.0
ratio_clamp = 20.0
BLOCK = 16
LANES = 128


def column_tiles(width):
    for tiles in (8, 4, 2, 1):
        if width % (LANES * tiles) == 0:
            return tiles


def stats_kernel(ids_ref, pol_ref, ref_ref, out_ref):
    width = pol_ref.shape[1]
    tiles = column_tiles(width)
    span = tiles * LANES
    steps = width // span
    low = jnp.full((BLOCK, LANES), -3.0e38, jnp.bfloat16)

    def peak_step(step, carry):
        top_p, top_q = carry
        for tile in range(tiles):
            at = pl.ds(pl.multiple_of(step * span + tile * LANES, LANES), LANES)
            top_p = jnp.maximum(top_p, pol_ref[:, at])
            top_q = jnp.maximum(top_q, ref_ref[:, at])
        return top_p, top_q

    top_p, top_q = lax.fori_loop(0, steps, peak_step, (low, low))
    peak_p = jnp.max(top_p.astype(jnp.float32), axis=1, keepdims=True)
    peak_q = jnp.max(top_q.astype(jnp.float32), axis=1, keepdims=True)
    wide_p = jnp.broadcast_to(peak_p, (BLOCK, LANES))
    wide_q = jnp.broadcast_to(peak_q, (BLOCK, LANES))
    lane = lax.broadcasted_iota(jnp.int32, (BLOCK, LANES), 1)
    wanted = ids_ref[...] - lane
    zero = jnp.zeros((BLOCK, LANES), jnp.float32)

    def sum_step(step, carry):
        total_p, cross, logit, total_q = carry
        for tile in range(tiles):
            first = step * span + tile * LANES
            at = pl.ds(pl.multiple_of(first, LANES), LANES)
            z = pol_ref[:, at].astype(jnp.float32)
            q = ref_ref[:, at].astype(jnp.float32)
            e = jnp.exp(z - wide_p)
            total_p = total_p + e
            cross = cross + e * (z - q)
            logit = logit + jnp.where(wanted == first, z, 0.0)
            total_q = total_q + jnp.exp(q - wide_q)
        return total_p, cross, logit, total_q

    sums = lax.fori_loop(0, steps, sum_step, (zero, zero, zero, zero))
    parts = [jnp.sum(part, axis=1, keepdims=True) for part in sums]
    out = zero
    for place, part in enumerate([peak_p, peak_q] + parts):
        out = jnp.where(lane == place, part, out)
    out_ref[...] = out


def grad_kernel(ids_ref, row_ref, pol_ref, ref_ref, out_ref):
    width = pol_ref.shape[1]
    tiles = column_tiles(width)
    span = tiles * LANES
    rows = row_ref[...]
    peak, slope, base, bump = (
        jnp.broadcast_to(rows[:, place : place + 1], (BLOCK, LANES)) for place in range(4)
    )
    lane = lax.broadcasted_iota(jnp.int32, (BLOCK, LANES), 1)
    wanted = ids_ref[...] - lane

    def step_body(step, carry):
        for tile in range(tiles):
            first = step * span + tile * LANES
            at = pl.ds(pl.multiple_of(first, LANES), LANES)
            z = pol_ref[:, at].astype(jnp.float32)
            q = ref_ref[:, at].astype(jnp.float32)
            grad = jnp.exp(z - peak) * (slope * (z - q) + base)
            grad = grad + jnp.where(wanted == first, bump, 0.0)
            out_ref[:, at] = grad.astype(jnp.bfloat16)
        return carry

    lax.fori_loop(0, width // span, step_body, 0)


def row_call(kernel, out_width, out_type, elements, ids, narrow, wide):
    slots, width = wide[0].shape
    block = lambda columns: pl.BlockSpec((BLOCK, columns), lambda step: (step, 0))
    ids = jnp.broadcast_to(ids[:, None], (slots, LANES))
    return pl.pallas_call(
        kernel,
        grid=(slots // BLOCK,),
        in_specs=[block(LANES)] * (1 + len(narrow)) + [block(width)] * len(wide),
        out_specs=block(out_width),
        out_shape=jax.ShapeDtypeStruct((slots, out_width), out_type),
        compiler_params=pltpu.CompilerParams(vmem_limit_bytes=24 * 1024 * 1024),
        cost_estimate=pl.CostEstimate(
            flops=elements * slots * width, bytes_accessed=6 * slots * width, transcendentals=0
        ),
    )(ids, *narrow, *wide)


def fetch_rows(ref_logits, rank, owner_of_row, owner_count, capacity):
    slot_count = owner_count * capacity
    send_slot = owner_of_row * capacity + rank
    picker = send_slot[None, :] == jnp.arange(slot_count)[:, None]
    sent_rows = jnp.dot(
        picker.astype(jnp.bfloat16), ref_logits, preferred_element_type=jnp.float32
    ).astype(jnp.bfloat16)
    got = lax.all_to_all(
        sent_rows.reshape(owner_count, capacity, -1),
        ("role", "dp"),
        split_axis=0,
        concat_axis=0,
        tiled=True,
    )
    return got.reshape(slot_count, -1)


def shards(ref_logits, token_ids, old_logp, owner_of_row, lengths, rewards, group_ids, pol_logits):
    role_count = lax.axis_size("role")
    data_count = lax.axis_size("dp")
    owner_count = role_count * data_count
    my_owner = lax.axis_index("role") * data_count + lax.axis_index("dp")
    row_count = ref_logits.shape[0]
    vocab_local = ref_logits.shape[1]
    slot_count = pol_logits.shape[0]
    capacity = slot_count // owner_count
    seq_count = rewards.shape[0]
    seq_local = lengths.shape[0]
    row_span = row_count // seq_local
    member = group_ids[:, None] == group_ids[None, :]
    group_total = jnp.sum(jnp.where(member, rewards[None, :], 0.0), axis=1)
    group_count = jnp.sum(member.astype(jnp.float32), axis=1)
    advantage = rewards - group_total / jnp.maximum(group_count, 1.0)

    row_index = jnp.arange(row_count)
    row_valid = row_index % row_span < jnp.repeat(lengths, row_span)
    local = jnp.stack(
        [owner_of_row * 2 + row_valid.astype(jnp.int32), token_ids], axis=0
    )
    every = lax.all_gather(local, ("role", "dp"), axis=0, tiled=False)
    every_old = lax.all_gather(old_logp, ("role", "dp"), axis=0, tiled=False)
    every_owner = every[:, 0] // 2
    every_valid = every[:, 0] % 2
    every_ids = every[:, 1]
    valid_total = jnp.sum(every_valid).astype(jnp.float32)
    same = owner_of_row[:, None] == owner_of_row[None, :]
    before = row_index[None, :] < row_index[:, None]
    rank = jnp.sum((same & before).astype(jnp.int32), axis=1)
    got_rows = fetch_rows(ref_logits, rank, owner_of_row, owner_count, capacity)

    mine = every_owner == my_owner
    my_rank = jnp.sum((mine[:, None, :] & before[None]).astype(jnp.int32), axis=2)
    slot_pos = jnp.arange(capacity)
    match = mine[:, None, :] & (my_rank[:, None, :] == slot_pos[None, :, None])
    take = lambda values: jnp.sum(jnp.where(match, values[:, None, :], 0), axis=2).reshape(slot_count)
    got_ids = take(every_ids)
    got_old = take(every_old.astype(jnp.float32))
    slot_valid = take(every_valid) > 0
    every_adv = jnp.repeat(advantage.reshape(owner_count, seq_local), row_span, axis=1)
    slot_adv = take(every_adv)
    near_ids = got_ids - lax.axis_index("tp") * vocab_local

    stats = row_call(
        stats_kernel, LANES, jnp.float32, 20, near_ids, (), (pol_logits, got_rows)
    )[:, :6]
    stats = lax.all_gather(stats.T, "tp", axis=0, tiled=False)
    near_p, near_q = stats[:, 0], stats[:, 1]
    peak_p = jnp.max(near_p, axis=0)
    peak_q = jnp.max(near_q, axis=0)
    shift_p = jnp.exp(near_p - peak_p)
    shift_q = jnp.exp(near_q - peak_q)
    total_p = jnp.sum(stats[:, 2] * shift_p, axis=0)
    cross_sum = jnp.sum(stats[:, 3] * shift_p, axis=0)
    token_logit = jnp.sum(stats[:, 4], axis=0)
    total_q = jnp.sum(stats[:, 5] * shift_q, axis=0)

    loss_scale = row_count * owner_count / valid_total
    log_p = peak_p + jnp.log(total_p)
    log_q = peak_q + jnp.log(total_q)
    mean_gap = cross_sum / total_p
    kl_term = mean_gap - log_p + log_q
    raw_log_ratio = token_logit - log_p - got_old
    prob_ratio = jnp.exp(jnp.clip(raw_log_ratio, -ratio_clamp, ratio_clamp))
    plain_loss = -slot_adv * prob_ratio
    clipped_loss = -slot_adv * jnp.clip(prob_ratio, low_bound, high_bound)
    upper_loss = jnp.maximum(plain_loss, clipped_loss)
    dual_loss = -dual_bound * slot_adv
    negative = slot_adv < 0.0
    policy_loss = jnp.where(negative, jnp.minimum(upper_loss, dual_loss), upper_loss)
    token_losses = jnp.where(slot_valid, policy_loss + kl_weight * kl_term, 0.0)
    inside = (prob_ratio > low_bound) & (prob_ratio < high_bound)
    token_coef = jnp.where((plain_loss >= clipped_loss) | inside, plain_loss, 0.0)
    token_coef = jnp.where(negative & (upper_loss > dual_loss), 0.0, token_coef)
    token_coef = jnp.where(jnp.abs(raw_log_ratio) < ratio_clamp, token_coef, 0.0)
    scale = jnp.where(slot_valid, loss_scale, 0.0)
    slope = scale * kl_weight / total_p
    base = -scale * (token_coef + kl_weight * mean_gap) / total_p
    bump = scale * token_coef
    per_row = jnp.stack([peak_p, slope, base, bump], axis=1)
    per_row = jnp.pad(per_row, ((0, 0), (0, LANES - 4)))
    grad_rows = row_call(
        grad_kernel, vocab_local, jnp.bfloat16, 10, near_ids, (per_row,), (pol_logits, got_rows)
    )
    return (grad_rows, token_losses)


def solution(mesh):
    return jax.shard_map(
        shards,
        mesh=mesh,
        in_specs=(
            P(("role", "dp"), "tp"),
            P(("role", "dp")),
            P(("role", "dp")),
            P(("role", "dp")),
            P(("role", "dp")),
            P(),
            P(),
            P(("role", "dp"), "tp"),
        ),
        out_specs=(P(("role", "dp"), "tp"), P(("role", "dp"))),
        check_vma=False,
    )
```

```python
import functools

import jax
import jax.numpy as jnp
from jax import lax
from jax.experimental import pallas as pl
from jax.experimental.pallas import tpu as pltpu
from jax.sharding import PartitionSpec as P

kl_weight = 0.04
low_bound = 0.8
high_bound = 1.2
dual_bound = 3.0
ratio_clamp = 20.0
BLOCK = 16
LANES = 128


def column_tiles(width):
    for tiles in (8, 4, 2, 1):
        if width % (LANES * tiles) == 0:
            return tiles


def stats_kernel(ids_ref, pol_ref, ref_ref, out_ref):
    width = pol_ref.shape[1]
    tiles = column_tiles(width)
    span = tiles * LANES
    steps = width // span
    low = jnp.full((BLOCK, LANES), -3.0e38, jnp.bfloat16)

    def peak_step(step, carry):
        top_p, top_q = carry
        for tile in range(tiles):
            at = pl.ds(pl.multiple_of(step * span + tile * LANES, LANES), LANES)
            top_p = jnp.maximum(top_p, pol_ref[:, at])
            top_q = jnp.maximum(top_q, ref_ref[:, at])
        return top_p, top_q

    top_p, top_q = lax.fori_loop(0, steps, peak_step, (low, low))
    peak_p = jnp.max(top_p.astype(jnp.float32), axis=1, keepdims=True)
    peak_q = jnp.max(top_q.astype(jnp.float32), axis=1, keepdims=True)
    wide_p = jnp.broadcast_to(peak_p, (BLOCK, LANES))
    wide_q = jnp.broadcast_to(peak_q, (BLOCK, LANES))
    lane = lax.broadcasted_iota(jnp.int32, (BLOCK, LANES), 1)
    wanted = ids_ref[...] - lane
    zero = jnp.zeros((BLOCK, LANES), jnp.float32)

    def sum_step(step, carry):
        total_p, cross, logit, total_q = carry
        for tile in range(tiles):
            first = step * span + tile * LANES
            at = pl.ds(pl.multiple_of(first, LANES), LANES)
            z = pol_ref[:, at].astype(jnp.float32)
            q = ref_ref[:, at].astype(jnp.float32)
            e = jnp.exp(z - wide_p)
            total_p = total_p + e
            cross = cross + e * (z - q)
            logit = logit + jnp.where(wanted == first, z, 0.0)
            total_q = total_q + jnp.exp(q - wide_q)
        return total_p, cross, logit, total_q

    sums = lax.fori_loop(0, steps, sum_step, (zero, zero, zero, zero))
    parts = [jnp.sum(part, axis=1, keepdims=True) for part in sums]
    out = zero
    for place, part in enumerate([peak_p, peak_q] + parts):
        out = jnp.where(lane == place, part, out)
    out_ref[...] = out


def grad_kernel(ids_ref, row_ref, pol_ref, ref_ref, out_ref):
    width = pol_ref.shape[1]
    tiles = column_tiles(width)
    span = tiles * LANES
    rows = row_ref[...]
    peak, slope, base, bump = (
        jnp.broadcast_to(rows[:, place : place + 1], (BLOCK, LANES)) for place in range(4)
    )
    lane = lax.broadcasted_iota(jnp.int32, (BLOCK, LANES), 1)
    wanted = ids_ref[...] - lane

    def step_body(step, carry):
        for tile in range(tiles):
            first = step * span + tile * LANES
            at = pl.ds(pl.multiple_of(first, LANES), LANES)
            z = pol_ref[:, at].astype(jnp.float32)
            q = ref_ref[:, at].astype(jnp.float32)
            grad = jnp.exp(z - peak) * (slope * (z - q) + base)
            grad = grad + jnp.where(wanted == first, bump, 0.0)
            out_ref[:, at] = grad.astype(jnp.bfloat16)
        return carry

    lax.fori_loop(0, width // span, step_body, 0)


def row_call(kernel, out_width, out_type, elements, ids, narrow, wide):
    slots, width = wide[0].shape
    block = lambda columns: pl.BlockSpec((BLOCK, columns), lambda step: (step, 0))
    ids = jnp.broadcast_to(ids[:, None], (slots, LANES))
    return pl.pallas_call(
        kernel,
        grid=(slots // BLOCK,),
        in_specs=[block(LANES)] * (1 + len(narrow)) + [block(width)] * len(wide),
        out_specs=block(out_width),
        out_shape=jax.ShapeDtypeStruct((slots, out_width), out_type),
        compiler_params=pltpu.CompilerParams(vmem_limit_bytes=24 * 1024 * 1024),
        cost_estimate=pl.CostEstimate(
            flops=elements * slots * width, bytes_accessed=6 * slots * width, transcendentals=0
        ),
    )(ids, *narrow, *wide)


def fetch_rows(ref_logits, rank, owner_of_row, owner_count, capacity):
    slot_count = owner_count * capacity
    send_slot = owner_of_row * capacity + rank
    picker = send_slot[None, :] == jnp.arange(slot_count)[:, None]
    sent_rows = jnp.dot(
        picker.astype(jnp.bfloat16), ref_logits, preferred_element_type=jnp.float32
    ).astype(jnp.bfloat16)
    got = lax.all_to_all(
        sent_rows.reshape(owner_count, capacity, -1),
        ("role", "dp"),
        split_axis=0,
        concat_axis=0,
        tiled=True,
    )
    return got.reshape(slot_count, -1)


LAGS = (0, 1, 3, 5)
CLASSES = ((64, 64, 64), (80, 80, 80), (96, 96, 96))


def route_kernel(
    caps, ids_ref, p0, p1a, p1b, p2a, p2b, fa, fb, ref_hbm, pol_hbm, out_hbm, stats_ref,
    pool, send0, send1, send2, pol, placed, acc, pol_sem, ref_sem, send_sem, recv_sem, out_sem,
):
    pieces, _, chunk = pool.shape
    steps = pieces // 2
    rows = ref_hbm.shape[0]
    slots = pol.shape[0]
    tiles = chunk // LANES
    role, core = lax.axis_index("role"), lax.axis_index("dp")
    side_x = {"role": role + 1 - 2 * lax.rem(role, 2)}
    side_y = {"role": lax.rem(role + 2, 4)}
    side_core = {"dp": 1 - core}
    targets = ((side_core, side_core), (side_x, side_y), (side_y, side_x))
    sends = (send0, send1, send2)
    pickers = ((p0, p0), (p1a, p1b), (p2a, p2b))
    tops = [rows]
    for cap in caps:
        tops.append(tops[-1] + cap)

    def first_column(piece):
        return pl.multiple_of(piece * chunk, LANES)

    def ref_copy(piece):
        return pltpu.make_async_copy(
            ref_hbm.at[:, pl.ds(first_column(piece), chunk)],
            pool.at[piece, pl.ds(0, rows)],
            ref_sem.at[piece],
        )

    def out_copy(piece):
        return pltpu.make_async_copy(
            placed.at[piece],
            out_hbm.at[:, pl.ds(first_column(piece), chunk)],
            out_sem.at[piece],
        )

    def hop(stage, side, step):
        piece = side * steps + step
        return pltpu.make_async_remote_copy(
            src_ref=sends[stage].at[piece],
            dst_ref=pool.at[piece, pl.ds(tops[stage], caps[stage])],
            send_sem=send_sem.at[stage, piece],
            recv_sem=recv_sem.at[stage, piece],
            device_id=targets[stage][side],
            device_id_type=pl.DeviceIdType.MESH,
        )

    def forward(stage, step):
        for side in range(2):
            piece = side * steps + step
            if stage == 0:
                ref_copy(piece).wait()
            else:
                hop(stage - 1, side, step).wait_recv()
            picked = jnp.dot(
                pickers[stage][side][...],
                pool[piece, pl.ds(0, tops[stage]), :],
                preferred_element_type=jnp.float32,
            )
            sends[stage][piece] = picked.astype(jnp.bfloat16)
            hop(stage, side, step).start()

    lane = lax.broadcasted_iota(jnp.int32, (BLOCK, LANES), 1)

    def finish(step):
        for side, picker in enumerate((fa, fb)):
            piece = side * steps + step
            hop(2, side, step).wait_recv()
            picked = jnp.dot(
                picker[...], pool[piece], preferred_element_type=jnp.float32
            )
            placed[piece] = picked.astype(jnp.bfloat16)
            out_copy(piece).start()

        def block_body(block, carry):
            at = pl.ds(pl.multiple_of(block * BLOCK, BLOCK), BLOCK)
            wanted = ids_ref[at, :] - lane
            zs, qs, firsts = [], [], []
            for side in range(2):
                piece = side * steps + step
                for tile in range(tiles):
                    first = pl.multiple_of(piece * chunk + tile * LANES, LANES)
                    zs.append(pol[at, pl.ds(first, LANES)].astype(jnp.float32))
                    qs.append(
                        placed[piece, at, pl.ds(tile * LANES, LANES)].astype(jnp.float32)
                    )
                    firsts.append(first)
            old_p, old_q = acc[0, at, :], acc[1, at, :]
            top_p = functools.reduce(jnp.maximum, zs, old_p)
            top_q = functools.reduce(jnp.maximum, qs, old_q)
            fade = jnp.exp(old_p - top_p)
            total_p, cross = acc[2, at, :] * fade, acc[3, at, :] * fade
            logit = acc[4, at, :]
            total_q = acc[5, at, :] * jnp.exp(old_q - top_q)
            for z, q, first in zip(zs, qs, firsts):
                e = jnp.exp(z - top_p)
                total_p = total_p + e
                cross = cross + e * (z - q)
                logit = logit + jnp.where(wanted == first, z, 0.0)
                total_q = total_q + jnp.exp(q - top_q)
            for place, part in enumerate((top_p, top_q, total_p, cross, logit, total_q)):
                acc[place, at, :] = part
            return carry

        lax.fori_loop(0, slots // BLOCK, block_body, 0)

    lax.fori_loop(0, pieces, lambda piece, c: (ref_copy(piece).start(), c)[1], 0)
    pol_copy = pltpu.make_async_copy(pol_hbm, pol, pol_sem)
    pol_copy.start()
    barrier = pltpu.get_barrier_semaphore()
    for partner in (side_core, side_x, side_y):
        pl.semaphore_signal(
            barrier, inc=1, device_id=partner, device_id_type=pl.DeviceIdType.MESH
        )
    acc[0:2] = jnp.full((2, slots, LANES), -3.0e38, jnp.float32)
    acc[2:6] = jnp.zeros((4, slots, LANES), jnp.float32)
    pl.semaphore_wait(barrier, 3)

    def segment(start, stop):
        active = [s for s in range(4) if LAGS[s] <= start and start - LAGS[s] < steps]

        def body(tick, carry):
            for stage in reversed(active):
                if stage < 3:
                    forward(stage, tick - LAGS[stage])
            if 3 in active:
                finish(tick - LAGS[3])
            return carry

        lax.fori_loop(start, stop, body, 0)

    edges = sorted(set(LAGS) | {lag + steps for lag in LAGS})
    for start, stop in zip(edges, edges[1:]):
        if start == LAGS[3]:
            pol_copy.wait()
        segment(start, stop)

    def drain(step, carry):
        for side in range(2):
            for stage in range(3):
                hop(stage, side, step).wait_send()
            out_copy(side * steps + step).wait()
        return carry

    lax.fori_loop(0, steps, drain, 0)

    def close(block, carry):
        at = pl.ds(pl.multiple_of(block * BLOCK, BLOCK), BLOCK)
        near_p, near_q = acc[0, at, :], acc[1, at, :]
        peak_p = jnp.max(near_p, axis=1, keepdims=True)
        peak_q = jnp.max(near_q, axis=1, keepdims=True)
        fade_p, fade_q = jnp.exp(near_p - peak_p), jnp.exp(near_q - peak_q)
        parts = [peak_p, peak_q]
        for place, fade in ((2, fade_p), (3, fade_p), (4, 1.0), (5, fade_q)):
            parts.append(jnp.sum(acc[place, at, :] * fade, axis=1, keepdims=True))
        out = jnp.zeros((BLOCK, LANES), jnp.float32)
        for place, part in enumerate(parts):
            out = jnp.where(lane == place, part, out)
        stats_ref[at, :] = out
        return carry

    lax.fori_loop(0, slots // BLOCK, close, 0)


def pick_plan(codes, mask, cap):
    count = codes.shape[-1]
    ahead = jnp.arange(count)[:, None] < jnp.arange(count)[None, :]
    place = jnp.dot(
        mask.astype(jnp.bfloat16), ahead.astype(jnp.bfloat16), preferred_element_type=jnp.float32
    ).astype(jnp.int32)
    place = jnp.where(mask, place, -1)
    chosen = place[:, None, :] == jnp.arange(cap)[None, :, None]
    return place, jnp.sum(jnp.where(chosen, codes[:, None, :], 0), axis=2)


def route(caps, place_id, codes, per_owner, me, ids, ref_logits, pol_logits):
    owner_count, rows = codes.shape
    slots, width = pol_logits.shape
    dev = jnp.arange(owner_count)[:, None]
    lane_of = lambda flip: lambda values: values[jnp.arange(owner_count) ^ flip]
    core, x, y = lane_of(1), lane_of(2), lane_of(4)

    def differs(values, bits):
        return ((((values - 1) // per_owner) ^ dev) & bits) != 0

    def live(values, same, other):
        return (values > 0) & ~differs(values, same) & differs(values, other)

    def picker(place, cap):
        mine = lax.dynamic_index_in_dim(place, me, 0, keepdims=False)
        return (mine[None, :] == jnp.arange(cap)[:, None]).astype(jnp.bfloat16)

    place, sent = pick_plan(codes, live(codes, 0, 1), caps[0])
    p0 = picker(place, caps[0])
    first = jnp.concatenate([codes, core(sent)], axis=1)
    plans, finals = [], []
    for turn, bits in ((x, 2), (y, 4)):
        back = 6 - bits
        place, sent = pick_plan(first, live(first, 1, bits), caps[1])
        p1 = picker(place, caps[1])
        second = jnp.concatenate([first, turn(sent)], axis=1)
        place, sent = pick_plan(second, live(second, 1 | bits, back), caps[2])
        p2 = picker(place, caps[2])
        third = jnp.concatenate([second, (y if bits == 2 else x)(sent)], axis=1)
        mine = lax.dynamic_index_in_dim(third, me, 0, keepdims=False)
        final = mine[None, :] - 1 - me * per_owner == jnp.arange(slots)[:, None]
        plans.append((p1, p2))
        finals.append(final.astype(jnp.bfloat16))

    chunk = LANES * next(t for t in (4, 2, 1) if width % (2 * LANES * t) == 0)
    pieces = width // chunk
    vmem = pl.BlockSpec(memory_space=pltpu.VMEM)
    anywhere = pl.BlockSpec(memory_space=pl.ANY)
    buffer = lambda count: pltpu.VMEM((pieces, count, chunk), jnp.bfloat16)
    return pl.pallas_call(
        functools.partial(route_kernel, caps),
        in_specs=[vmem] * 8 + [anywhere] * 2,
        out_specs=(anywhere, vmem),
        out_shape=(
            jax.ShapeDtypeStruct((slots, width), jnp.bfloat16),
            jax.ShapeDtypeStruct((slots, LANES), jnp.float32),
        ),
        scratch_shapes=[
            buffer(rows + sum(caps)),
            buffer(caps[0]),
            buffer(caps[1]),
            buffer(caps[2]),
            pltpu.VMEM((slots, width), jnp.bfloat16),
            buffer(slots),
            pltpu.VMEM((6, slots, LANES), jnp.float32),
            pltpu.SemaphoreType.DMA,
            pltpu.SemaphoreType.DMA((pieces,)),
            pltpu.SemaphoreType.DMA((3, pieces)),
            pltpu.SemaphoreType.DMA((3, pieces)),
            pltpu.SemaphoreType.DMA((pieces,)),
        ],
        compiler_params=pltpu.CompilerParams(
            collective_id=place_id, has_side_effects=True, vmem_limit_bytes=56 * 1024 * 1024
        ),
        cost_estimate=pl.CostEstimate(
            flops=40 * slots * width, bytes_accessed=6 * slots * width, transcendentals=0
        ),
    )(
        jnp.broadcast_to(ids[:, None], (slots, LANES)),
        p0, plans[0][0], plans[1][0], plans[0][1], plans[1][1], finals[0], finals[1],
        ref_logits, pol_logits,
    )


def needed(codes, per_owner):
    owner = jnp.where(codes > 0, (codes - 1) // per_owner, -1)
    counts = jnp.sum((owner[:, None, :] == jnp.arange(8)[None, :, None]).astype(jnp.int32), axis=2)
    counts = counts.reshape(2, 2, 2, 2, 2, 2)
    apart = 1 - jnp.eye(2, dtype=jnp.int32)
    worst = lambda text, out: jnp.max(jnp.sum(counts, axis=text) * apart.reshape(out))
    zero = worst((3, 4), (1, 1, 2, 2))
    one = jnp.maximum(worst((2, 3), (1, 2, 2, 1)), worst((2, 4), (2, 1, 2, 1)))
    two = jnp.maximum(worst((1, 2), (2, 2, 1, 1)), worst((0, 2), (2, 1, 2, 1)))
    return zero, one, two


def shards(ref_logits, token_ids, old_logp, owner_of_row, lengths, rewards, group_ids, pol_logits):
    role_count = lax.axis_size("role")
    data_count = lax.axis_size("dp")
    owner_count = role_count * data_count
    my_owner = lax.axis_index("role") * data_count + lax.axis_index("dp")
    row_count = ref_logits.shape[0]
    vocab_local = ref_logits.shape[1]
    slot_count = pol_logits.shape[0]
    capacity = slot_count // owner_count
    seq_count = rewards.shape[0]
    seq_local = lengths.shape[0]
    row_span = row_count // seq_local
    member = group_ids[:, None] == group_ids[None, :]
    group_total = jnp.sum(jnp.where(member, rewards[None, :], 0.0), axis=1)
    group_count = jnp.sum(member.astype(jnp.float32), axis=1)
    advantage = rewards - group_total / jnp.maximum(group_count, 1.0)

    row_index = jnp.arange(row_count)
    row_valid = row_index % row_span < jnp.repeat(lengths, row_span)
    local = jnp.stack(
        [owner_of_row * 2 + row_valid.astype(jnp.int32), token_ids], axis=0
    )
    every = lax.all_gather(local, ("role", "dp"), axis=0, tiled=False)
    every_old = lax.all_gather(old_logp, ("role", "dp"), axis=0, tiled=False)
    every_owner = every[:, 0] // 2
    every_valid = every[:, 0] % 2
    every_ids = every[:, 1]
    valid_total = jnp.sum(every_valid).astype(jnp.float32)
    before = row_index[None, :] < row_index[:, None]
    mine = every_owner == my_owner
    my_rank = jnp.sum((mine[:, None, :] & before[None]).astype(jnp.int32), axis=2)
    slot_pos = jnp.arange(capacity)
    match = mine[:, None, :] & (my_rank[:, None, :] == slot_pos[None, :, None])
    take = lambda values: jnp.sum(jnp.where(match, values[:, None, :], 0), axis=2).reshape(slot_count)
    got_ids = take(every_ids)
    got_old = take(every_old.astype(jnp.float32))
    slot_valid = take(every_valid) > 0
    every_adv = jnp.repeat(advantage.reshape(owner_count, seq_local), row_span, axis=1)
    slot_adv = take(every_adv)
    near_ids = got_ids - lax.axis_index("tp") * vocab_local

    if role_count == 4 and data_count == 2 and vocab_local % (2 * LANES) == 0:
        same = every_owner[:, :, None] == every_owner[:, None, :]
        every_rank = jnp.sum((same & before[None]).astype(jnp.int32), axis=2)
        block = jnp.arange(owner_count)[:, None]
        codes = every_owner * slot_count + block * capacity + every_rank + 1
        codes = jnp.where(every_valid > 0, codes, 0)
        need = needed(codes, slot_count)
        level = jnp.int32(0)
        for caps in CLASSES[:-1]:
            fits = [count <= cap for count, cap in zip(need, caps)]
            level = level + 1 - (fits[0] & fits[1] & fits[2]).astype(jnp.int32)
        branches = [
            lambda c, m, i, r, p, place=place, caps=caps: route(
                caps, 1 + place, c, slot_count, m, i, r, p
            )
            for place, caps in enumerate(CLASSES)
        ]
        got_rows, stats = lax.switch(
            level, branches, codes, my_owner, near_ids, ref_logits, pol_logits
        )
        stats = stats[:, :6]
    else:
        same = owner_of_row[:, None] == owner_of_row[None, :]
        rank = jnp.sum((same & before).astype(jnp.int32), axis=1)
        got_rows = fetch_rows(ref_logits, rank, owner_of_row, owner_count, capacity)
        stats = row_call(
            stats_kernel, LANES, jnp.float32, 20, near_ids, (), (pol_logits, got_rows)
        )[:, :6]
    stats = lax.all_gather(stats.T, "tp", axis=0, tiled=False)
    near_p, near_q = stats[:, 0], stats[:, 1]
    peak_p = jnp.max(near_p, axis=0)
    peak_q = jnp.max(near_q, axis=0)
    shift_p = jnp.exp(near_p - peak_p)
    shift_q = jnp.exp(near_q - peak_q)
    total_p = jnp.sum(stats[:, 2] * shift_p, axis=0)
    cross_sum = jnp.sum(stats[:, 3] * shift_p, axis=0)
    token_logit = jnp.sum(stats[:, 4], axis=0)
    total_q = jnp.sum(stats[:, 5] * shift_q, axis=0)

    loss_scale = row_count * owner_count / valid_total
    log_p = peak_p + jnp.log(total_p)
    log_q = peak_q + jnp.log(total_q)
    mean_gap = cross_sum / total_p
    kl_term = mean_gap - log_p + log_q
    raw_log_ratio = token_logit - log_p - got_old
    prob_ratio = jnp.exp(jnp.clip(raw_log_ratio, -ratio_clamp, ratio_clamp))
    plain_loss = -slot_adv * prob_ratio
    clipped_loss = -slot_adv * jnp.clip(prob_ratio, low_bound, high_bound)
    upper_loss = jnp.maximum(plain_loss, clipped_loss)
    dual_loss = -dual_bound * slot_adv
    negative = slot_adv < 0.0
    policy_loss = jnp.where(negative, jnp.minimum(upper_loss, dual_loss), upper_loss)
    token_losses = jnp.where(slot_valid, policy_loss + kl_weight * kl_term, 0.0)
    inside = (prob_ratio > low_bound) & (prob_ratio < high_bound)
    token_coef = jnp.where((plain_loss >= clipped_loss) | inside, plain_loss, 0.0)
    token_coef = jnp.where(negative & (upper_loss > dual_loss), 0.0, token_coef)
    token_coef = jnp.where(jnp.abs(raw_log_ratio) < ratio_clamp, token_coef, 0.0)
    scale = jnp.where(slot_valid, loss_scale, 0.0)
    slope = scale * kl_weight / total_p
    base = -scale * (token_coef + kl_weight * mean_gap) / total_p
    bump = scale * token_coef
    per_row = jnp.stack([peak_p, slope, base, bump], axis=1)
    per_row = jnp.pad(per_row, ((0, 0), (0, LANES - 4)))
    grad_rows = row_call(
        grad_kernel, vocab_local, jnp.bfloat16, 10, near_ids, (per_row,), (pol_logits, got_rows)
    )
    return (grad_rows, token_losses)


def solution(mesh):
    return jax.shard_map(
        shards,
        mesh=mesh,
        in_specs=(
            P(("role", "dp"), "tp"),
            P(("role", "dp")),
            P(("role", "dp")),
            P(("role", "dp")),
            P(("role", "dp")),
            P(),
            P(),
            P(("role", "dp"), "tp"),
        ),
        out_specs=(P(("role", "dp"), "tp"), P(("role", "dp"))),
        check_vma=False,
    )
```

```python
import functools

import jax
import jax.numpy as jnp
from jax import lax
from jax.experimental import pallas as pl
from jax.experimental.pallas import tpu as pltpu
from jax.sharding import PartitionSpec as P

kl_weight = 0.04
low_bound = 0.8
high_bound = 1.2
dual_bound = 3.0
ratio_clamp = 20.0
BLOCK = 16
LANES = 128


def column_tiles(width):
    for tiles in (8, 4, 2, 1):
        if width % (LANES * tiles) == 0:
            return tiles


def stats_kernel(ids_ref, pol_ref, ref_ref, out_ref):
    width = pol_ref.shape[1]
    tiles = column_tiles(width)
    span = tiles * LANES
    steps = width // span
    low = jnp.full((BLOCK, LANES), -3.0e38, jnp.bfloat16)

    def peak_step(step, carry):
        top_p, top_q = carry
        for tile in range(tiles):
            at = pl.ds(pl.multiple_of(step * span + tile * LANES, LANES), LANES)
            top_p = jnp.maximum(top_p, pol_ref[:, at])
            top_q = jnp.maximum(top_q, ref_ref[:, at])
        return top_p, top_q

    top_p, top_q = lax.fori_loop(0, steps, peak_step, (low, low))
    peak_p = jnp.max(top_p.astype(jnp.float32), axis=1, keepdims=True)
    peak_q = jnp.max(top_q.astype(jnp.float32), axis=1, keepdims=True)
    wide_p = jnp.broadcast_to(peak_p, (BLOCK, LANES))
    wide_q = jnp.broadcast_to(peak_q, (BLOCK, LANES))
    lane = lax.broadcasted_iota(jnp.int32, (BLOCK, LANES), 1)
    wanted = ids_ref[...] - lane
    zero = jnp.zeros((BLOCK, LANES), jnp.float32)

    def sum_step(step, carry):
        total_p, cross, logit, total_q = carry
        for tile in range(tiles):
            first = step * span + tile * LANES
            at = pl.ds(pl.multiple_of(first, LANES), LANES)
            z = pol_ref[:, at].astype(jnp.float32)
            q = ref_ref[:, at].astype(jnp.float32)
            e = jnp.exp(z - wide_p)
            total_p = total_p + e
            cross = cross + e * (z - q)
            logit = logit + jnp.where(wanted == first, z, 0.0)
            total_q = total_q + jnp.exp(q - wide_q)
        return total_p, cross, logit, total_q

    sums = lax.fori_loop(0, steps, sum_step, (zero, zero, zero, zero))
    parts = [jnp.sum(part, axis=1, keepdims=True) for part in sums]
    out = zero
    for place, part in enumerate([peak_p, peak_q] + parts):
        out = jnp.where(lane == place, part, out)
    out_ref[...] = out


def grad_kernel(ids_ref, row_ref, pol_ref, ref_ref, out_ref):
    width = pol_ref.shape[1]
    tiles = column_tiles(width)
    span = tiles * LANES
    rows = row_ref[...]
    peak, slope, base, bump = (
        jnp.broadcast_to(rows[:, place : place + 1], (BLOCK, LANES)) for place in range(4)
    )
    lane = lax.broadcasted_iota(jnp.int32, (BLOCK, LANES), 1)
    wanted = ids_ref[...] - lane

    def step_body(step, carry):
        for tile in range(tiles):
            first = step * span + tile * LANES
            at = pl.ds(pl.multiple_of(first, LANES), LANES)
            z = pol_ref[:, at].astype(jnp.float32)
            q = ref_ref[:, at].astype(jnp.float32)
            grad = jnp.exp(z - peak) * (slope * (z - q) + base)
            grad = grad + jnp.where(wanted == first, bump, 0.0)
            out_ref[:, at] = grad.astype(jnp.bfloat16)
        return carry

    lax.fori_loop(0, width // span, step_body, 0)


def row_call(kernel, out_width, out_type, elements, ids, narrow, wide):
    slots, width = wide[0].shape
    block = lambda columns: pl.BlockSpec((BLOCK, columns), lambda step: (step, 0))
    ids = jnp.broadcast_to(ids[:, None], (slots, LANES))
    return pl.pallas_call(
        kernel,
        grid=(slots // BLOCK,),
        in_specs=[block(LANES)] * (1 + len(narrow)) + [block(width)] * len(wide),
        out_specs=block(out_width),
        out_shape=jax.ShapeDtypeStruct((slots, out_width), out_type),
        compiler_params=pltpu.CompilerParams(vmem_limit_bytes=24 * 1024 * 1024),
        cost_estimate=pl.CostEstimate(
            flops=elements * slots * width, bytes_accessed=6 * slots * width, transcendentals=0
        ),
    )(ids, *narrow, *wide)


def fetch_rows(ref_logits, rank, owner_of_row, owner_count, capacity):
    slot_count = owner_count * capacity
    send_slot = owner_of_row * capacity + rank
    picker = send_slot[None, :] == jnp.arange(slot_count)[:, None]
    sent_rows = jnp.dot(
        picker.astype(jnp.bfloat16), ref_logits, preferred_element_type=jnp.float32
    ).astype(jnp.bfloat16)
    got = lax.all_to_all(
        sent_rows.reshape(owner_count, capacity, -1),
        ("role", "dp"),
        split_axis=0,
        concat_axis=0,
        tiled=True,
    )
    return got.reshape(slot_count, -1)


LAGS = (0, 1, 3, 5)
CLASSES = ((64, 64, 64), (80, 80, 80), (96, 96, 96))


def route_kernel(
    caps, ids_ref, where_ref, ref_hbm, pol_hbm, out_hbm, stats_ref,
    pool, send0, send1, send2, pol, placed, acc, spots, p0, p1, p2, final, near, shared,
    pol_sem, ref_sem, send_sem, recv_sem, out_sem, near_send, near_recv,
):
    pieces, _, chunk = pool.shape
    steps = pieces // 2
    rows = ref_hbm.shape[0]
    slots = pol.shape[0]
    tiles = chunk // LANES
    role, core = lax.axis_index("role"), lax.axis_index("dp")
    side_x = {"role": role + 1 - 2 * lax.rem(role, 2)}
    side_y = {"role": lax.rem(role + 2, 4)}
    side_core = {"dp": 1 - core}
    targets = ((side_core, side_core), (side_x, side_y), (side_y, side_x))
    sends = (send0, send1, send2)
    pickers = ((p0, p0), (p1.at[0], p1.at[1]), (p2.at[0], p2.at[1]))
    tp_size = lax.axis_size("tp")
    me_tp = lax.axis_index("tp")
    tops = [rows]
    for cap in caps:
        tops.append(tops[-1] + cap)

    def first_column(piece):
        return pl.multiple_of(piece * chunk, LANES)

    def ref_copy(piece):
        return pltpu.make_async_copy(
            ref_hbm.at[:, pl.ds(first_column(piece), chunk)],
            pool.at[piece, pl.ds(0, rows)],
            ref_sem.at[piece],
        )

    def out_copy(piece):
        return pltpu.make_async_copy(
            placed.at[piece],
            out_hbm.at[:, pl.ds(first_column(piece), chunk)],
            out_sem.at[piece],
        )

    def hop(stage, side, step):
        piece = side * steps + step
        return pltpu.make_async_remote_copy(
            src_ref=sends[stage].at[piece],
            dst_ref=pool.at[piece, pl.ds(tops[stage], caps[stage])],
            send_sem=send_sem.at[stage, piece],
            recv_sem=recv_sem.at[stage, piece],
            device_id=targets[stage][side],
            device_id_type=pl.DeviceIdType.MESH,
        )

    def forward(stage, step):
        for side in range(2):
            piece = side * steps + step
            if stage == 0:
                ref_copy(piece).wait()
            else:
                hop(stage - 1, side, step).wait_recv()
            picked = jnp.dot(
                pickers[stage][side][...],
                pool[piece, pl.ds(0, tops[stage]), :],
                preferred_element_type=jnp.float32,
            )
            sends[stage][piece] = picked.astype(jnp.bfloat16)
            hop(stage, side, step).start()

    lane = lax.broadcasted_iota(jnp.int32, (BLOCK, LANES), 1)

    def finish(step):
        for side, picker in enumerate((final.at[0], final.at[1])):
            piece = side * steps + step
            hop(2, side, step).wait_recv()
            picked = jnp.dot(
                picker[...], pool[piece], preferred_element_type=jnp.float32
            )
            placed[piece] = picked.astype(jnp.bfloat16)
            out_copy(piece).start()

        def block_body(block, carry):
            at = pl.ds(pl.multiple_of(block * BLOCK, BLOCK), BLOCK)
            wanted = ids_ref[at, :] - lane
            zs, qs, firsts = [], [], []
            for side in range(2):
                piece = side * steps + step
                for tile in range(tiles):
                    first = pl.multiple_of(piece * chunk + tile * LANES, LANES)
                    zs.append(pol[at, pl.ds(first, LANES)].astype(jnp.float32))
                    qs.append(
                        placed[piece, at, pl.ds(tile * LANES, LANES)].astype(jnp.float32)
                    )
                    firsts.append(first)
            old_p, old_q = acc[0, at, :], acc[1, at, :]
            top_p = functools.reduce(jnp.maximum, zs, old_p)
            top_q = functools.reduce(jnp.maximum, qs, old_q)
            fade = jnp.exp(old_p - top_p)
            total_p, cross = acc[2, at, :] * fade, acc[3, at, :] * fade
            logit = acc[4, at, :]
            total_q = acc[5, at, :] * jnp.exp(old_q - top_q)
            for z, q, first in zip(zs, qs, firsts):
                e = jnp.exp(z - top_p)
                total_p = total_p + e
                cross = cross + e * (z - q)
                logit = logit + jnp.where(wanted == first, z, 0.0)
                total_q = total_q + jnp.exp(q - top_q)
            for place, part in enumerate((top_p, top_q, total_p, cross, logit, total_q)):
                acc[place, at, :] = part
            return carry

        lax.fori_loop(0, slots // BLOCK, block_body, 0)

    lax.fori_loop(0, pieces, lambda piece, c: (ref_copy(piece).start(), c)[1], 0)
    pol_copy = pltpu.make_async_copy(pol_hbm, pol, pol_sem)
    pol_copy.start()
    barrier = pltpu.get_barrier_semaphore()
    peers = [{"tp": lax.rem(me_tp + hop_count, tp_size)} for hop_count in range(1, tp_size)]
    for partner in [side_core, side_x, side_y] + peers:
        pl.semaphore_signal(
            barrier, inc=1, device_id=partner, device_id_type=pl.DeviceIdType.MESH
        )
    acc[0:2] = jnp.full((2, slots, LANES), -3.0e38, jnp.float32)
    acc[2:6] = jnp.zeros((4, slots, LANES), jnp.float32)

    def hot(row, count):
        every = where_ref.shape[1]
        line = jnp.broadcast_to(where_ref[row : row + 1, :], (count, every))
        hit = line == lax.broadcasted_iota(jnp.int32, (count, every), 0)
        return jnp.where(hit, 1.0, 0.0).astype(jnp.bfloat16)

    def cross(picks, places):
        return lax.dot_general(
            picks, places, (((1,), (1,)), ((), ())), preferred_element_type=jnp.float32
        ).astype(jnp.bfloat16)

    for side in range(2):
        spots[side, 0:rows, :] = hot(0, rows)
        spots[side, rows : tops[1], :] = hot(2, caps[0])
        spots[side, tops[1] : tops[2], :] = hot(4 + 2 * side, caps[1])
        spots[side, tops[2] : tops[3], :] = hot(8 + 2 * side, caps[2])
        if side == 0:
            p0[...] = cross(hot(1, caps[0]), spots[0, 0:rows, :])
        p1[side] = cross(hot(3 + 2 * side, caps[1]), spots[side, 0 : tops[1], :])
        p2[side] = cross(hot(7 + 2 * side, caps[2]), spots[side, 0 : tops[2], :])
        final[side] = cross(hot(11, slots), spots[side])
    near[...] = jnp.zeros(near.shape, jnp.float32)
    pl.semaphore_wait(barrier, 2 + tp_size)

    def segment(start, stop):
        active = [s for s in range(4) if LAGS[s] <= start and start - LAGS[s] < steps]

        def body(tick, carry):
            for stage in reversed(active):
                if stage < 3:
                    forward(stage, tick - LAGS[stage])
            if 3 in active:
                finish(tick - LAGS[3])
            return carry

        lax.fori_loop(start, stop, body, 0)

    edges = sorted(set(LAGS) | {lag + steps for lag in LAGS})
    for start, stop in zip(edges, edges[1:]):
        if start == LAGS[3]:
            pol_copy.wait()
        segment(start, stop)

    def drain(step, carry):
        for side in range(2):
            for stage in range(3):
                hop(stage, side, step).wait_send()
            out_copy(side * steps + step).wait()
        return carry

    lax.fori_loop(0, steps, drain, 0)

    def close(block, carry):
        at = pl.ds(pl.multiple_of(block * BLOCK, BLOCK), BLOCK)
        near_p, near_q = acc[0, at, :], acc[1, at, :]
        peak_p = jnp.max(near_p, axis=1, keepdims=True)
        peak_q = jnp.max(near_q, axis=1, keepdims=True)
        fade_p, fade_q = jnp.exp(near_p - peak_p), jnp.exp(near_q - peak_q)
        parts = [peak_p, peak_q]
        for place, fade in ((2, fade_p), (3, fade_p), (4, 1.0), (5, fade_q)):
            parts.append(jnp.sum(acc[place, at, :] * fade, axis=1, keepdims=True))
        out = jnp.zeros((BLOCK, LANES), jnp.float32)
        for place, part in enumerate(parts):
            out = jnp.where(lane == place, part, out)
        near[at, :] = out
        return carry

    lax.fori_loop(0, slots // BLOCK, close, 0)
    shared[me_tp] = near[...].T[0:8, :]

    def share(away):
        return pltpu.make_async_remote_copy(
            src_ref=shared.at[me_tp],
            dst_ref=shared.at[me_tp],
            send_sem=near_send.at[away],
            recv_sem=near_recv.at[away],
            device_id={"tp": lax.rem(me_tp + away, tp_size)},
            device_id_type=pl.DeviceIdType.MESH,
        )

    for away in range(1, tp_size):
        share(away).start()
    for away in range(1, tp_size):
        share(away).wait_recv()
        share(away).wait_send()
    stats_ref[...] = shared[...]


def count_ahead(keys):
    count = keys.shape[1]
    ahead = jnp.arange(count)[None, :] < jnp.arange(count)[:, None]
    same = keys[:, :, None] == keys[:, None, :]
    return jnp.sum((same & ahead[None]).astype(jnp.int32), axis=2)


def hop_places(owner, valid, me, capacity, rows):
    every = jnp.arange(owner.shape[0])
    source = every // rows
    apart = source ^ owner
    core, x, y = (valid & ((apart & bit) != 0) for bit in (1, 2, 4))
    on_core = (source & 6) | (owner & 1)
    after_x = (source & 4) | (owner & 3)
    after_y = (source & 2) | (owner & 5)
    hops = ((core, source), (x, on_core), (y, on_core), (y, after_x), (x, after_y))
    keys = [jnp.where(crosses, key, -1) for crosses, key in hops]
    keys = jnp.stack(keys + [source * 8 + owner])
    ahead = count_ahead(keys)
    lines = [jnp.where(source == me, every % rows, -1)]
    for place, turn in enumerate((1, 2, 4, 4, 2)):
        lines.append(jnp.where(keys[place] == me, ahead[place], -1))
        lines.append(jnp.where(keys[place] == me ^ turn, ahead[place], -1))
    slot = source * capacity + ahead[5]
    lines.append(jnp.where(valid & (owner == me), slot, -1))
    lines += [jnp.full_like(every, -1)] * 4
    most = jnp.max(jnp.where(keys[:5] >= 0, ahead[:5] + 1, 0), axis=1)
    need = (most[0], jnp.maximum(most[1], most[2]), jnp.maximum(most[3], most[4]))
    return jnp.stack(lines).astype(jnp.int32), need, ahead[5]


def route(caps, place_id, places, ids, ref_logits, pol_logits):
    rows = ref_logits.shape[0]
    slots, width = pol_logits.shape
    every = places.shape[1]
    tp_size = lax.axis_size("tp")
    chunk = LANES * next(t for t in (4, 2, 1) if width % (2 * LANES * t) == 0)
    pieces = width // chunk
    padded = -(-slots // LANES) * LANES
    vmem = pl.BlockSpec(memory_space=pltpu.VMEM)
    anywhere = pl.BlockSpec(memory_space=pl.ANY)
    kept = lambda *shape: pltpu.VMEM(shape, jnp.bfloat16)
    buffer = lambda count: kept(pieces, count, chunk)
    full = rows + sum(caps)
    return pl.pallas_call(
        functools.partial(route_kernel, caps),
        in_specs=[vmem] * 2 + [anywhere] * 2,
        out_specs=(anywhere, vmem),
        out_shape=(
            jax.ShapeDtypeStruct((slots, width), jnp.bfloat16),
            jax.ShapeDtypeStruct((tp_size, 8, padded), jnp.float32),
        ),
        scratch_shapes=[
            buffer(full),
            buffer(caps[0]),
            buffer(caps[1]),
            buffer(caps[2]),
            kept(slots, width),
            buffer(slots),
            pltpu.VMEM((6, slots, LANES), jnp.float32),
            kept(2, full, every),
            kept(caps[0], rows),
            kept(2, caps[1], rows + caps[0]),
            kept(2, caps[2], rows + caps[0] + caps[1]),
            kept(2, slots, full),
            pltpu.VMEM((padded, LANES), jnp.float32),
            pltpu.VMEM((tp_size, 8, padded), jnp.float32),
            pltpu.SemaphoreType.DMA,
            pltpu.SemaphoreType.DMA((pieces,)),
            pltpu.SemaphoreType.DMA((3, pieces)),
            pltpu.SemaphoreType.DMA((3, pieces)),
            pltpu.SemaphoreType.DMA((pieces,)),
            pltpu.SemaphoreType.DMA((tp_size,)),
            pltpu.SemaphoreType.DMA((tp_size,)),
        ],
        compiler_params=pltpu.CompilerParams(
            collective_id=place_id, has_side_effects=True, vmem_limit_bytes=56 * 1024 * 1024
        ),
        cost_estimate=pl.CostEstimate(
            flops=40 * slots * width, bytes_accessed=6 * slots * width, transcendentals=0
        ),
    )(jnp.broadcast_to(ids[:, None], (slots, LANES)), places, ref_logits, pol_logits)


def shards(ref_logits, token_ids, old_logp, owner_of_row, lengths, rewards, group_ids, pol_logits):
    role_count = lax.axis_size("role")
    data_count = lax.axis_size("dp")
    owner_count = role_count * data_count
    my_owner = lax.axis_index("role") * data_count + lax.axis_index("dp")
    row_count = ref_logits.shape[0]
    vocab_local = ref_logits.shape[1]
    slot_count = pol_logits.shape[0]
    capacity = slot_count // owner_count
    seq_count = rewards.shape[0]
    seq_local = lengths.shape[0]
    row_span = row_count // seq_local
    member = group_ids[:, None] == group_ids[None, :]
    group_total = jnp.sum(jnp.where(member, rewards[None, :], 0.0), axis=1)
    group_count = jnp.sum(member.astype(jnp.float32), axis=1)
    advantage = rewards - group_total / jnp.maximum(group_count, 1.0)

    row_index = jnp.arange(row_count)
    row_valid = row_index % row_span < jnp.repeat(lengths, row_span)
    tag = owner_of_row * 2 + row_valid.astype(jnp.int32)
    local = jnp.stack([part.astype(jnp.float32) for part in (tag, token_ids, old_logp)])
    every = lax.all_gather(local, ("role", "dp"), axis=0, tiled=False)
    every_tag = every[:, 0].astype(jnp.int32)
    every_owner = every_tag // 2
    every_valid = every_tag % 2
    every_ids = every[:, 1].astype(jnp.int32)
    every_old = every[:, 2]
    valid_total = jnp.sum(every_valid).astype(jnp.float32)
    before = row_index[None, :] < row_index[:, None]
    mine = every_owner == my_owner
    my_rank = jnp.sum((mine[:, None, :] & before[None]).astype(jnp.int32), axis=2)
    slot_pos = jnp.arange(capacity)
    match = mine[:, None, :] & (my_rank[:, None, :] == slot_pos[None, :, None])
    take = lambda values: jnp.sum(jnp.where(match, values[:, None, :], 0), axis=2).reshape(slot_count)
    got_ids = take(every_ids)
    got_old = take(every_old)
    slot_valid = take(every_valid) > 0
    every_adv = jnp.repeat(advantage.reshape(owner_count, seq_local), row_span, axis=1)
    slot_adv = take(every_adv)
    near_ids = got_ids - lax.axis_index("tp") * vocab_local

    if role_count == 4 and data_count == 2 and vocab_local % (2 * LANES) == 0:
        places, need, _ = hop_places(
            every_owner.reshape(-1), every_valid.reshape(-1) > 0, my_owner, capacity, row_count
        )
        level = jnp.int32(0)
        for caps in CLASSES[:-1]:
            fits = [count <= cap for count, cap in zip(need, caps)]
            level = level + 1 - (fits[0] & fits[1] & fits[2]).astype(jnp.int32)
        branches = [
            functools.partial(route, caps, 1 + place) for place, caps in enumerate(CLASSES)
        ]
        got_rows, stats = lax.switch(
            level, branches, places, near_ids, ref_logits, pol_logits
        )
        stats = stats[:, :6, :slot_count]
    else:
        same = owner_of_row[:, None] == owner_of_row[None, :]
        rank = jnp.sum((same & before).astype(jnp.int32), axis=1)
        got_rows = fetch_rows(ref_logits, rank, owner_of_row, owner_count, capacity)
        stats = row_call(
            stats_kernel, LANES, jnp.float32, 20, near_ids, (), (pol_logits, got_rows)
        )[:, :6]
        stats = lax.all_gather(stats.T, "tp", axis=0, tiled=False)
    near_p, near_q = stats[:, 0], stats[:, 1]
    peak_p = jnp.max(near_p, axis=0)
    peak_q = jnp.max(near_q, axis=0)
    shift_p = jnp.exp(near_p - peak_p)
    shift_q = jnp.exp(near_q - peak_q)
    total_p = jnp.sum(stats[:, 2] * shift_p, axis=0)
    cross_sum = jnp.sum(stats[:, 3] * shift_p, axis=0)
    token_logit = jnp.sum(stats[:, 4], axis=0)
    total_q = jnp.sum(stats[:, 5] * shift_q, axis=0)

    loss_scale = row_count * owner_count / valid_total
    log_p = peak_p + jnp.log(total_p)
    log_q = peak_q + jnp.log(total_q)
    mean_gap = cross_sum / total_p
    kl_term = mean_gap - log_p + log_q
    raw_log_ratio = token_logit - log_p - got_old
    prob_ratio = jnp.exp(jnp.clip(raw_log_ratio, -ratio_clamp, ratio_clamp))
    plain_loss = -slot_adv * prob_ratio
    clipped_loss = -slot_adv * jnp.clip(prob_ratio, low_bound, high_bound)
    upper_loss = jnp.maximum(plain_loss, clipped_loss)
    dual_loss = -dual_bound * slot_adv
    negative = slot_adv < 0.0
    policy_loss = jnp.where(negative, jnp.minimum(upper_loss, dual_loss), upper_loss)
    token_losses = jnp.where(slot_valid, policy_loss + kl_weight * kl_term, 0.0)
    inside = (prob_ratio > low_bound) & (prob_ratio < high_bound)
    token_coef = jnp.where((plain_loss >= clipped_loss) | inside, plain_loss, 0.0)
    token_coef = jnp.where(negative & (upper_loss > dual_loss), 0.0, token_coef)
    token_coef = jnp.where(jnp.abs(raw_log_ratio) < ratio_clamp, token_coef, 0.0)
    scale = jnp.where(slot_valid, loss_scale, 0.0)
    slope = scale * kl_weight / total_p
    base = -scale * (token_coef + kl_weight * mean_gap) / total_p
    bump = scale * token_coef
    per_row = jnp.stack([peak_p, slope, base, bump], axis=1)
    per_row = jnp.pad(per_row, ((0, 0), (0, LANES - 4)))
    grad_rows = row_call(
        grad_kernel, vocab_local, jnp.bfloat16, 10, near_ids, (per_row,), (pol_logits, got_rows)
    )
    return (grad_rows, token_losses)


def solution(mesh):
    return jax.shard_map(
        shards,
        mesh=mesh,
        in_specs=(
            P(("role", "dp"), "tp"),
            P(("role", "dp")),
            P(("role", "dp")),
            P(("role", "dp")),
            P(("role", "dp")),
            P(),
            P(),
            P(("role", "dp"), "tp"),
        ),
        out_specs=(P(("role", "dp"), "tp"), P(("role", "dp"))),
        check_vma=False,
    )
```

```python
import functools

import jax
import jax.numpy as jnp
from jax import lax
from jax.experimental import pallas as pl
from jax.experimental.pallas import tpu as pltpu
from jax.sharding import PartitionSpec as P

kl_weight = 0.04
low_bound = 0.8
high_bound = 1.2
dual_bound = 3.0
ratio_clamp = 20.0
BLOCK = 16
LANES = 128


def column_tiles(width):
    for tiles in (38, 19, 8, 4, 2, 1):
        if width % (LANES * tiles) == 0:
            return tiles


def stats_kernel(ids_ref, pol_ref, ref_ref, out_ref):
    width = pol_ref.shape[1]
    tiles = column_tiles(width)
    span = tiles * LANES
    steps = width // span
    low = jnp.full((BLOCK, LANES), -3.0e38, jnp.bfloat16)

    def peak_step(step, carry):
        top_p, top_q = carry
        for tile in range(tiles):
            at = pl.ds(pl.multiple_of(step * span + tile * LANES, LANES), LANES)
            top_p = jnp.maximum(top_p, pol_ref[:, at])
            top_q = jnp.maximum(top_q, ref_ref[:, at])
        return top_p, top_q

    top_p, top_q = lax.fori_loop(0, steps, peak_step, (low, low))
    peak_p = jnp.max(top_p.astype(jnp.float32), axis=1, keepdims=True)
    peak_q = jnp.max(top_q.astype(jnp.float32), axis=1, keepdims=True)
    wide_p = jnp.broadcast_to(peak_p, (BLOCK, LANES))
    wide_q = jnp.broadcast_to(peak_q, (BLOCK, LANES))
    lane = lax.broadcasted_iota(jnp.int32, (BLOCK, LANES), 1)
    wanted = ids_ref[...] - lane
    zero = jnp.zeros((BLOCK, LANES), jnp.float32)

    def sum_step(step, carry):
        total_p, cross, logit, total_q = carry
        for tile in range(tiles):
            first = step * span + tile * LANES
            at = pl.ds(pl.multiple_of(first, LANES), LANES)
            z = pol_ref[:, at].astype(jnp.float32)
            q = ref_ref[:, at].astype(jnp.float32)
            e = jnp.exp(z - wide_p)
            total_p = total_p + e
            cross = cross + e * (z - q)
            logit = logit + jnp.where(wanted == first, z, 0.0)
            total_q = total_q + jnp.exp(q - wide_q)
        return total_p, cross, logit, total_q

    sums = lax.fori_loop(0, steps, sum_step, (zero, zero, zero, zero))
    parts = [jnp.sum(part, axis=1, keepdims=True) for part in sums]
    out = zero
    for place, part in enumerate([peak_p, peak_q] + parts):
        out = jnp.where(lane == place, part, out)
    out_ref[...] = out


def grad_kernel(ids_ref, row_ref, pol_ref, ref_ref, out_ref):
    width = pol_ref.shape[1]
    tiles = column_tiles(width)
    span = tiles * LANES
    rows = row_ref[...]
    peak, slope, base, bump = (
        jnp.broadcast_to(rows[:, place : place + 1], (BLOCK, LANES)) for place in range(4)
    )
    lane = lax.broadcasted_iota(jnp.int32, (BLOCK, LANES), 1)
    wanted = ids_ref[...] - lane

    def step_body(step, carry):
        for tile in range(tiles):
            first = step * span + tile * LANES
            at = pl.ds(pl.multiple_of(first, LANES), LANES)
            z = pol_ref[:, at].astype(jnp.float32)
            q = ref_ref[:, at].astype(jnp.float32)
            grad = jnp.exp(z - peak) * (slope * (z - q) + base)
            grad = grad + jnp.where(wanted == first, bump, 0.0)
            out_ref[:, at] = grad.astype(jnp.bfloat16)
        return carry

    lax.fori_loop(0, width // span, step_body, 0)


def row_call(kernel, out_width, out_type, elements, ids, narrow, wide):
    slots, width = wide[0].shape
    block = lambda columns: pl.BlockSpec((BLOCK, columns), lambda step: (step, 0))
    ids = jnp.broadcast_to(ids[:, None], (slots, LANES))
    return pl.pallas_call(
        kernel,
        grid=(slots // BLOCK,),
        in_specs=[block(LANES)] * (1 + len(narrow)) + [block(width)] * len(wide),
        out_specs=block(out_width),
        out_shape=jax.ShapeDtypeStruct((slots, out_width), out_type),
        compiler_params=pltpu.CompilerParams(vmem_limit_bytes=24 * 1024 * 1024),
        cost_estimate=pl.CostEstimate(
            flops=elements * slots * width, bytes_accessed=6 * slots * width, transcendentals=0
        ),
    )(ids, *narrow, *wide)


def fetch_rows(ref_logits, rank, owner_of_row, owner_count, capacity):
    slot_count = owner_count * capacity
    send_slot = owner_of_row * capacity + rank
    picker = send_slot[None, :] == jnp.arange(slot_count)[:, None]
    sent_rows = jnp.dot(
        picker.astype(jnp.bfloat16), ref_logits, preferred_element_type=jnp.float32
    ).astype(jnp.bfloat16)
    got = lax.all_to_all(
        sent_rows.reshape(owner_count, capacity, -1),
        ("role", "dp"),
        split_axis=0,
        concat_axis=0,
        tiled=True,
    )
    return got.reshape(slot_count, -1)


LAGS = (0, 1, 3, 5)
CLASSES = ((96, 64, 48), (96, 64, 64), (96, 64, 80), (96, 80, 80), (96, 96, 96))


def route_kernel(
    caps, ids_ref, where_ref, ref_hbm, pol_hbm, out_hbm, stats_ref,
    pool, send0, send1, send2, pol, placed, acc, spots, p0, p1, p2, final, near, shared,
    pol_sem, ref_sem, send_sem, recv_sem, out_sem, near_send, near_recv,
):
    pieces, _, chunk = pool.shape
    steps = pieces // 2
    rows = ref_hbm.shape[0]
    slots = pol.shape[0]
    tiles = chunk // LANES
    role, core = lax.axis_index("role"), lax.axis_index("dp")
    side_x = {"role": role + 1 - 2 * lax.rem(role, 2)}
    side_y = {"role": lax.rem(role + 2, 4)}
    side_core = {"dp": 1 - core}
    targets = ((side_core, side_core), (side_x, side_y), (side_y, side_x))
    sends = (send0, send1, send2)
    pickers = ((p0, p0), (p1.at[0], p1.at[1]), (p2.at[0], p2.at[1]))
    tp_size = lax.axis_size("tp")
    me_tp = lax.axis_index("tp")
    tops = [rows]
    for cap in caps:
        tops.append(tops[-1] + cap)

    def first_column(piece):
        return pl.multiple_of(piece * chunk, LANES)

    def ref_copy(piece):
        return pltpu.make_async_copy(
            ref_hbm.at[:, pl.ds(first_column(piece), chunk)],
            pool.at[piece, pl.ds(0, rows)],
            ref_sem.at[piece],
        )

    def out_copy(piece):
        return pltpu.make_async_copy(
            placed.at[piece],
            out_hbm.at[:, pl.ds(first_column(piece), chunk)],
            out_sem.at[piece],
        )

    def hop(stage, side, step):
        piece = side * steps + step
        return pltpu.make_async_remote_copy(
            src_ref=sends[stage].at[piece],
            dst_ref=pool.at[piece, pl.ds(tops[stage], caps[stage])],
            send_sem=send_sem.at[stage, piece],
            recv_sem=recv_sem.at[stage, piece],
            device_id=targets[stage][side],
            device_id_type=pl.DeviceIdType.MESH,
        )

    def forward(stage, step):
        for side in range(2):
            piece = side * steps + step
            if stage == 0:
                ref_copy(piece).wait()
            else:
                hop(stage - 1, side, step).wait_recv()
            picked = jnp.dot(
                pickers[stage][side][...],
                pool[piece, pl.ds(0, tops[stage]), :],
                preferred_element_type=jnp.float32,
            )
            sends[stage][piece] = picked.astype(jnp.bfloat16)
            hop(stage, side, step).start()

    lane = lax.broadcasted_iota(jnp.int32, (BLOCK, LANES), 1)

    def finish(step):
        for side, picker in enumerate((final.at[0], final.at[1])):
            piece = side * steps + step
            hop(2, side, step).wait_recv()
            picked = jnp.dot(
                picker[...], pool[piece], preferred_element_type=jnp.float32
            )
            placed[piece] = picked.astype(jnp.bfloat16)
            out_copy(piece).start()

        group = next(size for size in (4, 3, 2, 1) if slots // BLOCK % size == 0)

        def group_body(place, carry):
            for block in range(group):
                block_body(place * group + block)
            return carry

        def block_body(block):
            at = pl.ds(pl.multiple_of(block * BLOCK, BLOCK), BLOCK)
            wanted = ids_ref[at, :] - lane
            zs, qs, firsts = [], [], []
            for side in range(2):
                piece = side * steps + step
                for tile in range(tiles):
                    first = pl.multiple_of(piece * chunk + tile * LANES, LANES)
                    zs.append(pol[at, pl.ds(first, LANES)].astype(jnp.float32))
                    qs.append(
                        placed[piece, at, pl.ds(tile * LANES, LANES)].astype(jnp.float32)
                    )
                    firsts.append(first)
            old_p, old_q = acc[0, at, :], acc[1, at, :]
            top_p = functools.reduce(jnp.maximum, zs, old_p)
            top_q = functools.reduce(jnp.maximum, qs, old_q)
            fade = jnp.exp(old_p - top_p)
            total_p, cross = acc[2, at, :] * fade, acc[3, at, :] * fade
            logit = acc[4, at, :]
            total_q = acc[5, at, :] * jnp.exp(old_q - top_q)
            for z, q, first in zip(zs, qs, firsts):
                e = jnp.exp(z - top_p)
                total_p = total_p + e
                cross = cross + e * (z - q)
                logit = logit + jnp.where(wanted == first, z, 0.0)
                total_q = total_q + jnp.exp(q - top_q)
            for place, part in enumerate((top_p, top_q, total_p, cross, logit, total_q)):
                acc[place, at, :] = part

        lax.fori_loop(0, slots // BLOCK // group, group_body, 0)


    def fetch(step, carry):
        ref_copy(step).start()
        ref_copy(steps + step).start()
        return carry

    lax.fori_loop(0, steps, fetch, 0)
    pol_copy = pltpu.make_async_copy(pol_hbm, pol, pol_sem)
    pol_copy.start()
    barrier = pltpu.get_barrier_semaphore()
    peers = [{"tp": lax.rem(me_tp + hop_count, tp_size)} for hop_count in range(1, tp_size)]
    for partner in [side_core, side_x, side_y] + peers:
        pl.semaphore_signal(
            barrier, inc=1, device_id=partner, device_id_type=pl.DeviceIdType.MESH
        )
    acc[0:2] = jnp.full((2, slots, LANES), -3.0e38, jnp.float32)
    acc[2:6] = jnp.zeros((4, slots, LANES), jnp.float32)

    def hot(row, count):
        every = where_ref.shape[1]
        line = jnp.broadcast_to(where_ref[row : row + 1, :], (count, every))
        hit = line == lax.broadcasted_iota(jnp.int32, (count, every), 0)
        return jnp.where(hit, 1.0, 0.0).astype(jnp.bfloat16)

    def cross(picks, places):
        return lax.dot_general(
            picks, places, (((1,), (1,)), ((), ())), preferred_element_type=jnp.float32
        ).astype(jnp.bfloat16)

    def prepare(stage):
        count = slots if stage == 3 else caps[stage]
        for side in range(1 if stage == 0 else 2):
            both = 2 * side if stage in (1, 2) else 0
            if side == 0 or stage < 3:
                picks = hot((1, 3, 7, 11)[stage] + both, count)
            if stage < 2 and side == 1:
                pass
            elif stage == 0:
                spots[0, 0:rows, :] = hot(0, rows)
            elif stage == 1:
                spots[0, rows : tops[1], :] = hot(2, caps[0])
            else:
                low, row = tops[stage - 1], 4 * (stage - 1) + 2 * side
                spots[side, low : tops[stage], :] = hot(row, caps[stage - 1])
            low = min(tops[1], tops[stage])
            target = (p0, p1, p2, final)[stage]
            target = target if stage == 0 else target.at[side]
            target[:, 0:low] = cross(picks, spots[0, 0:low, :])
            if stage > 1:
                target[:, low : tops[stage]] = cross(picks, spots[side, low : tops[stage], :])

    prepare(0)
    near[...] = jnp.zeros(near.shape, jnp.float32)
    pl.semaphore_wait(barrier, 2 + tp_size)

    def segment(start, stop):
        active = [s for s in range(4) if LAGS[s] <= start and start - LAGS[s] < steps]

        def body(tick, carry):
            for stage in reversed(active):
                if stage < 3:
                    forward(stage, tick - LAGS[stage])
            if 3 in active:
                finish(tick - LAGS[3])
            return carry

        lax.fori_loop(start, stop, body, 0)

    edges = sorted(set(LAGS) | {lag + steps for lag in LAGS})
    for start, stop in zip(edges, edges[1:]):
        if start in LAGS[1:]:
            prepare(LAGS.index(start))
        if start == LAGS[3]:
            pol_copy.wait()
        segment(start, stop)

    def drain(step, carry):
        for side in range(2):
            for stage in range(3):
                hop(stage, side, step).wait_send()
            out_copy(side * steps + step).wait()
        return carry

    lax.fori_loop(0, steps, drain, 0)

    def close(block, carry):
        at = pl.ds(pl.multiple_of(block * BLOCK, BLOCK), BLOCK)
        near_p, near_q = acc[0, at, :], acc[1, at, :]
        peak_p = jnp.max(near_p, axis=1, keepdims=True)
        peak_q = jnp.max(near_q, axis=1, keepdims=True)
        fade_p, fade_q = jnp.exp(near_p - peak_p), jnp.exp(near_q - peak_q)
        parts = [peak_p, peak_q]
        for place, fade in ((2, fade_p), (3, fade_p), (4, 1.0), (5, fade_q)):
            parts.append(jnp.sum(acc[place, at, :] * fade, axis=1, keepdims=True))
        out = jnp.zeros((BLOCK, LANES), jnp.float32)
        for place, part in enumerate(parts):
            out = jnp.where(lane == place, part, out)
        near[at, :] = out
        return carry

    lax.fori_loop(0, slots // BLOCK, close, 0)
    shared[me_tp] = near[...].T[0:8, :]

    def share(away):
        return pltpu.make_async_remote_copy(
            src_ref=shared.at[me_tp],
            dst_ref=shared.at[me_tp],
            send_sem=near_send.at[away],
            recv_sem=near_recv.at[away],
            device_id={"tp": lax.rem(me_tp + away, tp_size)},
            device_id_type=pl.DeviceIdType.MESH,
        )

    for away in range(1, tp_size):
        share(away).start()
    for away in range(1, tp_size):
        share(away).wait_recv()
        share(away).wait_send()
    stats_ref[...] = shared[...]


def count_ahead(keys, kinds):
    count = keys[0].shape[0]
    ahead = jnp.arange(count)[:, None] < jnp.arange(count)[None, :]
    hot = [key[None, :] == jnp.arange(kind)[:, None] for key, kind in zip(keys, kinds)]
    every = jnp.concatenate(hot, axis=0)
    sums = jnp.dot(
        every.astype(jnp.bfloat16), ahead.astype(jnp.bfloat16), preferred_element_type=jnp.float32
    )
    sums = jnp.where(every, sums, 0.0)
    out, first = [], 0
    for kind in kinds:
        out.append(jnp.sum(sums[first : first + kind], axis=0))
        first += kind
    return jnp.stack(out).astype(jnp.int32)


def hop_places(owner, valid, me, capacity, rows):
    every = jnp.arange(owner.shape[0])
    source = every // rows
    apart = source ^ owner
    core, x, y = (valid & ((apart & bit) != 0) for bit in (1, 2, 4))
    on_core = (source & 6) | (owner & 1)
    after_x = (source & 4) | (owner & 3)
    after_y = (source & 2) | (owner & 5)
    hops = ((core, source), (x, on_core), (y, on_core), (y, after_x), (x, after_y))
    keys = [jnp.where(crosses, key, -1) for crosses, key in hops]
    ahead = count_ahead(keys + [source * 8 + owner], [8] * 5 + [64])
    keys = jnp.stack(keys)
    lines = [jnp.where(source == me, every % rows, -1)]
    for place, turn in enumerate((1, 2, 4, 4, 2)):
        lines.append(jnp.where(keys[place] == me, ahead[place], -1))
        lines.append(jnp.where(keys[place] == me ^ turn, ahead[place], -1))
    slot = source * capacity + ahead[5]
    lines.append(jnp.where(valid & (owner == me), slot, -1))
    lines += [jnp.full_like(every, -1)] * 4
    most = jnp.max(jnp.where(keys >= 0, ahead[:5] + 1, 0), axis=1)
    need = (most[0], jnp.maximum(most[1], most[2]), jnp.maximum(most[3], most[4]))
    return jnp.stack(lines).astype(jnp.int32), need, ahead[5]


def route(caps, place_id, places, ids, ref_logits, pol_logits):
    rows = ref_logits.shape[0]
    slots, width = pol_logits.shape
    every = places.shape[1]
    tp_size = lax.axis_size("tp")
    chunk = LANES * next(t for t in (4, 2, 1) if width % (2 * LANES * t) == 0)
    pieces = width // chunk
    padded = -(-slots // LANES) * LANES
    vmem = pl.BlockSpec(memory_space=pltpu.VMEM)
    anywhere = pl.BlockSpec(memory_space=pl.ANY)
    kept = lambda *shape: pltpu.VMEM(shape, jnp.bfloat16)
    buffer = lambda count: kept(pieces, count, chunk)
    full = rows + sum(caps)
    return pl.pallas_call(
        functools.partial(route_kernel, caps),
        in_specs=[vmem] * 2 + [anywhere] * 2,
        out_specs=(anywhere, vmem),
        out_shape=(
            jax.ShapeDtypeStruct((slots, width), jnp.bfloat16),
            jax.ShapeDtypeStruct((tp_size, 8, padded), jnp.float32),
        ),
        scratch_shapes=[
            buffer(full),
            buffer(caps[0]),
            buffer(caps[1]),
            buffer(caps[2]),
            kept(slots, width),
            buffer(slots),
            pltpu.VMEM((6, slots, LANES), jnp.float32),
            kept(2, full, every),
            kept(caps[0], rows),
            kept(2, caps[1], rows + caps[0]),
            kept(2, caps[2], rows + caps[0] + caps[1]),
            kept(2, slots, full),
            pltpu.VMEM((padded, LANES), jnp.float32),
            pltpu.VMEM((tp_size, 8, padded), jnp.float32),
            pltpu.SemaphoreType.DMA,
            pltpu.SemaphoreType.DMA((pieces,)),
            pltpu.SemaphoreType.DMA((3, pieces)),
            pltpu.SemaphoreType.DMA((3, pieces)),
            pltpu.SemaphoreType.DMA((pieces,)),
            pltpu.SemaphoreType.DMA((tp_size,)),
            pltpu.SemaphoreType.DMA((tp_size,)),
        ],
        compiler_params=pltpu.CompilerParams(
            collective_id=place_id, has_side_effects=True, vmem_limit_bytes=56 * 1024 * 1024
        ),
        cost_estimate=pl.CostEstimate(
            flops=40 * slots * width, bytes_accessed=6 * slots * width, transcendentals=0
        ),
    )(jnp.broadcast_to(ids[:, None], (slots, LANES)), places, ref_logits, pol_logits)


def shards(ref_logits, token_ids, old_logp, owner_of_row, lengths, rewards, group_ids, pol_logits):
    role_count = lax.axis_size("role")
    data_count = lax.axis_size("dp")
    owner_count = role_count * data_count
    my_owner = lax.axis_index("role") * data_count + lax.axis_index("dp")
    row_count = ref_logits.shape[0]
    vocab_local = ref_logits.shape[1]
    slot_count = pol_logits.shape[0]
    capacity = slot_count // owner_count
    seq_count = rewards.shape[0]
    seq_local = lengths.shape[0]
    row_span = row_count // seq_local
    member = group_ids[:, None] == group_ids[None, :]
    group_total = jnp.sum(jnp.where(member, rewards[None, :], 0.0), axis=1)
    group_count = jnp.sum(member.astype(jnp.float32), axis=1)
    advantage = rewards - group_total / jnp.maximum(group_count, 1.0)

    row_index = jnp.arange(row_count)
    row_valid = row_index % row_span < jnp.repeat(lengths, row_span)
    tag = owner_of_row * 2 + row_valid.astype(jnp.int32)
    local = jnp.stack([part.astype(jnp.float32) for part in (tag, token_ids, old_logp)])
    every = lax.all_gather(local, ("role", "dp"), axis=0, tiled=False)
    every_tag = every[:, 0].astype(jnp.int32)
    every_owner = every_tag // 2
    every_valid = every_tag % 2
    every_ids = every[:, 1].astype(jnp.int32)
    every_old = every[:, 2]
    valid_total = jnp.sum(every_valid).astype(jnp.float32)
    before = row_index[None, :] < row_index[:, None]
    mine = every_owner == my_owner
    my_rank = jnp.sum((mine[:, None, :] & before[None]).astype(jnp.int32), axis=2)
    slot_pos = jnp.arange(capacity)
    match = mine[:, None, :] & (my_rank[:, None, :] == slot_pos[None, :, None])
    take = lambda values: jnp.sum(jnp.where(match, values[:, None, :], 0), axis=2).reshape(slot_count)
    got_ids = take(every_ids)
    got_old = take(every_old)
    slot_valid = take(every_valid) > 0
    every_adv = jnp.repeat(advantage.reshape(owner_count, seq_local), row_span, axis=1)
    slot_adv = take(every_adv)
    near_ids = got_ids - lax.axis_index("tp") * vocab_local

    if role_count == 4 and data_count == 2 and vocab_local % (2 * LANES) == 0:
        places, need, _ = hop_places(
            every_owner.reshape(-1), every_valid.reshape(-1) > 0, my_owner, capacity, row_count
        )
        level = jnp.int32(0)
        for caps in CLASSES[:-1]:
            fits = [count <= cap for count, cap in zip(need, caps)]
            level = level + 1 - (fits[0] & fits[1] & fits[2]).astype(jnp.int32)
        branches = [
            functools.partial(route, caps, 1 + place) for place, caps in enumerate(CLASSES)
        ]
        got_rows, stats = lax.switch(
            level, branches, places, near_ids, ref_logits, pol_logits
        )
        stats = stats[:, :6, :slot_count]
    else:
        same = owner_of_row[:, None] == owner_of_row[None, :]
        rank = jnp.sum((same & before).astype(jnp.int32), axis=1)
        got_rows = fetch_rows(ref_logits, rank, owner_of_row, owner_count, capacity)
        stats = row_call(
            stats_kernel, LANES, jnp.float32, 20, near_ids, (), (pol_logits, got_rows)
        )[:, :6]
        stats = lax.all_gather(stats.T, "tp", axis=0, tiled=False)
    near_p, near_q = stats[:, 0], stats[:, 1]
    peak_p = jnp.max(near_p, axis=0)
    peak_q = jnp.max(near_q, axis=0)
    shift_p = jnp.exp(near_p - peak_p)
    shift_q = jnp.exp(near_q - peak_q)
    total_p = jnp.sum(stats[:, 2] * shift_p, axis=0)
    cross_sum = jnp.sum(stats[:, 3] * shift_p, axis=0)
    token_logit = jnp.sum(stats[:, 4], axis=0)
    total_q = jnp.sum(stats[:, 5] * shift_q, axis=0)

    loss_scale = row_count * owner_count / valid_total
    log_p = peak_p + jnp.log(total_p)
    log_q = peak_q + jnp.log(total_q)
    mean_gap = cross_sum / total_p
    kl_term = mean_gap - log_p + log_q
    raw_log_ratio = token_logit - log_p - got_old
    prob_ratio = jnp.exp(jnp.clip(raw_log_ratio, -ratio_clamp, ratio_clamp))
    plain_loss = -slot_adv * prob_ratio
    clipped_loss = -slot_adv * jnp.clip(prob_ratio, low_bound, high_bound)
    upper_loss = jnp.maximum(plain_loss, clipped_loss)
    dual_loss = -dual_bound * slot_adv
    negative = slot_adv < 0.0
    policy_loss = jnp.where(negative, jnp.minimum(upper_loss, dual_loss), upper_loss)
    token_losses = jnp.where(slot_valid, policy_loss + kl_weight * kl_term, 0.0)
    inside = (prob_ratio > low_bound) & (prob_ratio < high_bound)
    token_coef = jnp.where((plain_loss >= clipped_loss) | inside, plain_loss, 0.0)
    token_coef = jnp.where(negative & (upper_loss > dual_loss), 0.0, token_coef)
    token_coef = jnp.where(jnp.abs(raw_log_ratio) < ratio_clamp, token_coef, 0.0)
    scale = jnp.where(slot_valid, loss_scale, 0.0)
    slope = scale * kl_weight / total_p
    base = -scale * (token_coef + kl_weight * mean_gap) / total_p
    bump = scale * token_coef
    per_row = jnp.stack([peak_p, slope, base, bump], axis=1)
    per_row = jnp.pad(per_row, ((0, 0), (0, LANES - 4)))
    grad_rows = row_call(
        grad_kernel, vocab_local, jnp.bfloat16, 10, near_ids, (per_row,), (pol_logits, got_rows)
    )
    return (grad_rows, token_losses)


def solution(mesh):
    return jax.shard_map(
        shards,
        mesh=mesh,
        in_specs=(
            P(("role", "dp"), "tp"),
            P(("role", "dp")),
            P(("role", "dp")),
            P(("role", "dp")),
            P(("role", "dp")),
            P(),
            P(),
            P(("role", "dp"), "tp"),
        ),
        out_specs=(P(("role", "dp"), "tp"), P(("role", "dp"))),
        check_vma=False,
    )
```

```python
import functools

import jax
import jax.numpy as jnp
from jax import lax
from jax.experimental import pallas as pl
from jax.experimental.pallas import tpu as pltpu
from jax.sharding import PartitionSpec as P

kl_weight = 0.04
low_bound = 0.8
high_bound = 1.2
dual_bound = 3.0
ratio_clamp = 20.0
BLOCK = 16
LANES = 128


def column_tiles(width):
    for tiles in (38, 19, 8, 4, 2, 1):
        if width % (LANES * tiles) == 0:
            return tiles


def stats_kernel(ids_ref, pol_ref, ref_ref, out_ref):
    width = pol_ref.shape[1]
    tiles = column_tiles(width)
    span = tiles * LANES
    steps = width // span
    low = jnp.full((BLOCK, LANES), -3.0e38, jnp.bfloat16)

    def peak_step(step, carry):
        top_p, top_q = carry
        for tile in range(tiles):
            at = pl.ds(pl.multiple_of(step * span + tile * LANES, LANES), LANES)
            top_p = jnp.maximum(top_p, pol_ref[:, at])
            top_q = jnp.maximum(top_q, ref_ref[:, at])
        return top_p, top_q

    top_p, top_q = lax.fori_loop(0, steps, peak_step, (low, low))
    peak_p = jnp.max(top_p.astype(jnp.float32), axis=1, keepdims=True)
    peak_q = jnp.max(top_q.astype(jnp.float32), axis=1, keepdims=True)
    wide_p = jnp.broadcast_to(peak_p, (BLOCK, LANES))
    wide_q = jnp.broadcast_to(peak_q, (BLOCK, LANES))
    lane = lax.broadcasted_iota(jnp.int32, (BLOCK, LANES), 1)
    wanted = ids_ref[...] - lane
    zero = jnp.zeros((BLOCK, LANES), jnp.float32)

    def sum_step(step, carry):
        total_p, cross, logit, total_q = carry
        for tile in range(tiles):
            first = step * span + tile * LANES
            at = pl.ds(pl.multiple_of(first, LANES), LANES)
            z = pol_ref[:, at].astype(jnp.float32)
            q = ref_ref[:, at].astype(jnp.float32)
            e = jnp.exp(z - wide_p)
            total_p = total_p + e
            cross = cross + e * (z - q)
            logit = logit + jnp.where(wanted == first, z, 0.0)
            total_q = total_q + jnp.exp(q - wide_q)
        return total_p, cross, logit, total_q

    sums = lax.fori_loop(0, steps, sum_step, (zero, zero, zero, zero))
    parts = [jnp.sum(part, axis=1, keepdims=True) for part in sums]
    out = zero
    for place, part in enumerate([peak_p, peak_q] + parts):
        out = jnp.where(lane == place, part, out)
    out_ref[...] = out


def grad_kernel(ids_ref, row_ref, pol_ref, ref_ref, out_ref):
    width = pol_ref.shape[1]
    tiles = column_tiles(width)
    span = tiles * LANES
    rows = row_ref[...]
    peak, slope, base, bump = (
        jnp.broadcast_to(rows[:, place : place + 1], (BLOCK, LANES)) for place in range(4)
    )
    lane = lax.broadcasted_iota(jnp.int32, (BLOCK, LANES), 1)
    wanted = ids_ref[...] - lane

    def step_body(step, carry):
        for tile in range(tiles):
            first = step * span + tile * LANES
            at = pl.ds(pl.multiple_of(first, LANES), LANES)
            z = pol_ref[:, at].astype(jnp.float32)
            q = ref_ref[:, at].astype(jnp.float32)
            grad = jnp.exp(z - peak) * (slope * (z - q) + base)
            grad = grad + jnp.where(wanted == first, bump, 0.0)
            out_ref[:, at] = grad.astype(jnp.bfloat16)
        return carry

    lax.fori_loop(0, width // span, step_body, 0)


def row_call(kernel, out_width, out_type, elements, ids, narrow, wide):
    slots, width = wide[0].shape
    block = lambda columns: pl.BlockSpec((BLOCK, columns), lambda step: (step, 0))
    ids = jnp.broadcast_to(ids[:, None], (slots, LANES))
    return pl.pallas_call(
        kernel,
        grid=(slots // BLOCK,),
        in_specs=[block(LANES)] * (1 + len(narrow)) + [block(width)] * len(wide),
        out_specs=block(out_width),
        out_shape=jax.ShapeDtypeStruct((slots, out_width), out_type),
        compiler_params=pltpu.CompilerParams(vmem_limit_bytes=24 * 1024 * 1024),
        cost_estimate=pl.CostEstimate(
            flops=elements * slots * width, bytes_accessed=6 * slots * width, transcendentals=0
        ),
    )(ids, *narrow, *wide)


def fetch_rows(ref_logits, rank, owner_of_row, owner_count, capacity):
    slot_count = owner_count * capacity
    send_slot = owner_of_row * capacity + rank
    picker = send_slot[None, :] == jnp.arange(slot_count)[:, None]
    sent_rows = jnp.dot(
        picker.astype(jnp.bfloat16), ref_logits, preferred_element_type=jnp.float32
    ).astype(jnp.bfloat16)
    got = lax.all_to_all(
        sent_rows.reshape(owner_count, capacity, -1),
        ("role", "dp"),
        split_axis=0,
        concat_axis=0,
        tiled=True,
    )
    return got.reshape(slot_count, -1)


LAGS = (0, 1, 3, 5)
CLASSES = ((96, 64, 48), (96, 64, 64), (96, 64, 80), (96, 80, 80), (96, 96, 96))


def route_kernel(
    caps, ids_ref, where_ref, ref_hbm, pol_hbm, out_hbm, stats_ref,
    pool, send0, send1, send2, pol, placed, acc, spots, p0, p1, p2, final, near, shared,
    pol_sem, ref_sem, send_sem, recv_sem, out_sem, near_send, near_recv,
):
    pieces, _, chunk = pool.shape
    steps = pieces // 2
    rows = ref_hbm.shape[0]
    slots = pol.shape[0]
    tiles = chunk // LANES
    role, core = lax.axis_index("role"), lax.axis_index("dp")
    side_x = {"role": role + 1 - 2 * lax.rem(role, 2)}
    side_y = {"role": lax.rem(role + 2, 4)}
    side_core = {"dp": 1 - core}
    targets = ((side_core, side_core), (side_x, side_y), (side_y, side_x))
    sends = (send0, send1, send2)
    pickers = ((p0, p0), (p1.at[0], p1.at[1]), (p2.at[0], p2.at[1]))
    tp_size = lax.axis_size("tp")
    me_tp = lax.axis_index("tp")
    tops = [rows]
    for cap in caps:
        tops.append(tops[-1] + cap)

    def first_column(piece):
        return pl.multiple_of(piece * chunk, LANES)

    def ref_copy(piece):
        return pltpu.make_async_copy(
            ref_hbm.at[:, pl.ds(first_column(piece), chunk)],
            pool.at[piece, pl.ds(0, rows)],
            ref_sem.at[piece],
        )

    def out_copy(piece):
        return pltpu.make_async_copy(
            placed.at[piece],
            out_hbm.at[:, pl.ds(first_column(piece), chunk)],
            out_sem.at[piece],
        )

    def hop(stage, side, step):
        piece = side * steps + step
        return pltpu.make_async_remote_copy(
            src_ref=sends[stage].at[piece],
            dst_ref=pool.at[piece, pl.ds(tops[stage], caps[stage])],
            send_sem=send_sem.at[stage, piece],
            recv_sem=recv_sem.at[stage, piece],
            device_id=targets[stage][side],
            device_id_type=pl.DeviceIdType.MESH,
        )

    def forward(stage, step):
        for side in range(2):
            piece = side * steps + step
            if stage == 0:
                ref_copy(piece).wait()
            else:
                hop(stage - 1, side, step).wait_recv()
            picked = jnp.dot(
                pickers[stage][side][...],
                pool[piece, pl.ds(0, tops[stage]), :],
                preferred_element_type=jnp.float32,
            )
            sends[stage][piece] = picked.astype(jnp.bfloat16)
            hop(stage, side, step).start()

    lane = lax.broadcasted_iota(jnp.int32, (BLOCK, LANES), 1)

    def finish(step):
        for side, picker in enumerate((final.at[0], final.at[1])):
            piece = side * steps + step
            hop(2, side, step).wait_recv()
            picked = jnp.dot(
                picker[...], pool[piece], preferred_element_type=jnp.float32
            )
            placed[piece] = picked.astype(jnp.bfloat16)
            out_copy(piece).start()

        group = next(size for size in (4, 3, 2, 1) if slots // BLOCK % size == 0)

        def group_body(place, carry):
            for block in range(group):
                block_body(place * group + block)
            return carry

        def block_body(block):
            at = pl.ds(pl.multiple_of(block * BLOCK, BLOCK), BLOCK)
            wanted = ids_ref[at, :] - lane
            zs, qs, firsts = [], [], []
            for side in range(2):
                piece = side * steps + step
                for tile in range(tiles):
                    first = pl.multiple_of(piece * chunk + tile * LANES, LANES)
                    zs.append(pol[at, pl.ds(first, LANES)].astype(jnp.float32))
                    qs.append(
                        placed[piece, at, pl.ds(tile * LANES, LANES)].astype(jnp.float32)
                    )
                    firsts.append(first)
            old_p, old_q = acc[0, at, :], acc[1, at, :]
            top_p = functools.reduce(jnp.maximum, zs, old_p)
            top_q = functools.reduce(jnp.maximum, qs, old_q)
            fade = jnp.exp(old_p - top_p)
            total_p, cross = acc[2, at, :] * fade, acc[3, at, :] * fade
            logit = acc[4, at, :]
            total_q = acc[5, at, :] * jnp.exp(old_q - top_q)
            for z, q, first in zip(zs, qs, firsts):
                e = jnp.exp(z - top_p)
                total_p = total_p + e
                cross = cross + e * (z - q)
                logit = logit + jnp.where(wanted == first, z, 0.0)
                total_q = total_q + jnp.exp(q - top_q)
            for place, part in enumerate((top_p, top_q, total_p, cross, logit, total_q)):
                acc[place, at, :] = part

        lax.fori_loop(0, slots // BLOCK // group, group_body, 0)


    def fetch(step, carry):
        ref_copy(step).start()
        ref_copy(steps + step).start()
        return carry

    lax.fori_loop(0, steps, fetch, 0)
    pol_copy = pltpu.make_async_copy(pol_hbm, pol, pol_sem)
    pol_copy.start()
    barrier = pltpu.get_barrier_semaphore()
    peers = [{"tp": lax.rem(me_tp + hop_count, tp_size)} for hop_count in range(1, tp_size)]
    for partner in [side_core, side_x, side_y] + peers:
        pl.semaphore_signal(
            barrier, inc=1, device_id=partner, device_id_type=pl.DeviceIdType.MESH
        )
    acc[0:2] = jnp.full((2, slots, LANES), -3.0e38, jnp.float32)
    acc[2:6] = jnp.zeros((4, slots, LANES), jnp.float32)

    def hot(row, count):
        every = where_ref.shape[1]
        line = jnp.broadcast_to(where_ref[row : row + 1, :], (count, every))
        hit = line == lax.broadcasted_iota(jnp.int32, (count, every), 0)
        return jnp.where(hit, 1.0, 0.0).astype(jnp.bfloat16)

    def cross(picks, places):
        return lax.dot_general(
            picks, places, (((1,), (1,)), ((), ())), preferred_element_type=jnp.float32
        ).astype(jnp.bfloat16)

    def prepare(stage):
        count = slots if stage == 3 else caps[stage]
        for side in range(1 if stage == 0 else 2):
            both = 2 * side if stage in (1, 2) else 0
            if side == 0 or stage < 3:
                picks = hot((1, 3, 7, 11)[stage] + both, count)
            if stage < 2 and side == 1:
                pass
            elif stage == 0:
                spots[0, 0:rows, :] = hot(0, rows)
            elif stage == 1:
                spots[0, rows : tops[1], :] = hot(2, caps[0])
            else:
                low, row = tops[stage - 1], 4 * (stage - 1) + 2 * side
                spots[side, low : tops[stage], :] = hot(row, caps[stage - 1])
            low = min(tops[1], tops[stage])
            target = (p0, p1, p2, final)[stage]
            target = target if stage == 0 else target.at[side]
            target[:, 0:low] = cross(picks, spots[0, 0:low, :])
            if stage > 1:
                target[:, low : tops[stage]] = cross(picks, spots[side, low : tops[stage], :])

    prepare(0)
    near[...] = jnp.zeros(near.shape, jnp.float32)
    pl.semaphore_wait(barrier, 2 + tp_size)

    def segment(start, stop):
        active = [s for s in range(4) if LAGS[s] <= start and start - LAGS[s] < steps]

        def body(tick, carry):
            for stage in reversed(active):
                if stage < 3:
                    forward(stage, tick - LAGS[stage])
            if 3 in active:
                finish(tick - LAGS[3])
            return carry

        lax.fori_loop(start, stop, body, 0)

    edges = sorted(set(LAGS) | {lag + steps for lag in LAGS})
    for start, stop in zip(edges, edges[1:]):
        if start in LAGS[1:]:
            prepare(LAGS.index(start))
        if start == LAGS[3]:
            pol_copy.wait()
        segment(start, stop)

    def drain(step, carry):
        for side in range(2):
            for stage in range(3):
                hop(stage, side, step).wait_send()
            out_copy(side * steps + step).wait()
        return carry

    lax.fori_loop(0, steps, drain, 0)

    def close(block, carry):
        at = pl.ds(pl.multiple_of(block * BLOCK, BLOCK), BLOCK)
        near_p, near_q = acc[0, at, :], acc[1, at, :]
        peak_p = jnp.max(near_p, axis=1, keepdims=True)
        peak_q = jnp.max(near_q, axis=1, keepdims=True)
        fade_p, fade_q = jnp.exp(near_p - peak_p), jnp.exp(near_q - peak_q)
        parts = [peak_p, peak_q]
        for place, fade in ((2, fade_p), (3, fade_p), (4, 1.0), (5, fade_q)):
            parts.append(jnp.sum(acc[place, at, :] * fade, axis=1, keepdims=True))
        out = jnp.zeros((BLOCK, LANES), jnp.float32)
        for place, part in enumerate(parts):
            out = jnp.where(lane == place, part, out)
        near[at, :] = out
        return carry

    lax.fori_loop(0, slots // BLOCK, close, 0)
    shared[me_tp] = near[...].T[0:8, :]

    def share(away):
        return pltpu.make_async_remote_copy(
            src_ref=shared.at[me_tp],
            dst_ref=shared.at[me_tp],
            send_sem=near_send.at[away],
            recv_sem=near_recv.at[away],
            device_id={"tp": lax.rem(me_tp + away, tp_size)},
            device_id_type=pl.DeviceIdType.MESH,
        )

    for away in range(1, tp_size):
        share(away).start()
    for away in range(1, tp_size):
        share(away).wait_recv()
        share(away).wait_send()
    stats_ref[...] = shared[...]


def count_ahead(keys, kinds):
    count = keys[0].shape[0]
    ahead = jnp.arange(count)[:, None] < jnp.arange(count)[None, :]
    hot = [key[None, :] == jnp.arange(kind)[:, None] for key, kind in zip(keys, kinds)]
    every = jnp.concatenate(hot, axis=0)
    sums = jnp.dot(
        every.astype(jnp.bfloat16), ahead.astype(jnp.bfloat16), preferred_element_type=jnp.float32
    )
    sums = jnp.where(every, sums, 0.0)
    out, first = [], 0
    for kind in kinds:
        out.append(jnp.sum(sums[first : first + kind], axis=0))
        first += kind
    return jnp.stack(out).astype(jnp.int32)


def hop_places(owner, valid, me, capacity, rows):
    every = jnp.arange(owner.shape[0])
    source = every // rows
    apart = source ^ owner
    core, x, y = (valid & ((apart & bit) != 0) for bit in (1, 2, 4))
    on_core = (source & 6) | (owner & 1)
    after_x = (source & 4) | (owner & 3)
    after_y = (source & 2) | (owner & 5)
    hops = ((core, source), (x, on_core), (y, on_core), (y, after_x), (x, after_y))
    keys = [jnp.where(crosses, key, -1) for crosses, key in hops]
    ahead = count_ahead(keys + [source * 8 + owner], [8] * 5 + [64])
    keys = jnp.stack(keys)
    lines = [jnp.where(source == me, every % rows, -1)]
    for place, turn in enumerate((1, 2, 4, 4, 2)):
        lines.append(jnp.where(keys[place] == me, ahead[place], -1))
        lines.append(jnp.where(keys[place] == me ^ turn, ahead[place], -1))
    slot = source * capacity + ahead[5]
    lines.append(jnp.where(valid & (owner == me), slot, -1))
    lines += [jnp.full_like(every, -1)] * 4
    most = jnp.max(jnp.where(keys >= 0, ahead[:5] + 1, 0), axis=1)
    need = (most[0], jnp.maximum(most[1], most[2]), jnp.maximum(most[3], most[4]))
    return jnp.stack(lines).astype(jnp.int32), need, ahead[5]


def route(caps, place_id, places, ids, ref_logits, pol_logits):
    rows = ref_logits.shape[0]
    slots, width = pol_logits.shape
    every = places.shape[1]
    tp_size = lax.axis_size("tp")
    chunk = LANES * next(t for t in (2, 1) if width % (2 * LANES * t) == 0)
    pieces = width // chunk
    padded = -(-slots // LANES) * LANES
    vmem = pl.BlockSpec(memory_space=pltpu.VMEM)
    anywhere = pl.BlockSpec(memory_space=pl.ANY)
    kept = lambda *shape: pltpu.VMEM(shape, jnp.bfloat16)
    buffer = lambda count: kept(pieces, count, chunk)
    full = rows + sum(caps)
    return pl.pallas_call(
        functools.partial(route_kernel, caps),
        in_specs=[vmem] * 2 + [anywhere] * 2,
        out_specs=(anywhere, vmem),
        out_shape=(
            jax.ShapeDtypeStruct((slots, width), jnp.bfloat16),
            jax.ShapeDtypeStruct((tp_size, 8, padded), jnp.float32),
        ),
        scratch_shapes=[
            buffer(full),
            buffer(caps[0]),
            buffer(caps[1]),
            buffer(caps[2]),
            kept(slots, width),
            buffer(slots),
            pltpu.VMEM((6, slots, LANES), jnp.float32),
            kept(2, full, every),
            kept(caps[0], rows),
            kept(2, caps[1], rows + caps[0]),
            kept(2, caps[2], rows + caps[0] + caps[1]),
            kept(2, slots, full),
            pltpu.VMEM((padded, LANES), jnp.float32),
            pltpu.VMEM((tp_size, 8, padded), jnp.float32),
            pltpu.SemaphoreType.DMA,
            pltpu.SemaphoreType.DMA((pieces,)),
            pltpu.SemaphoreType.DMA((3, pieces)),
            pltpu.SemaphoreType.DMA((3, pieces)),
            pltpu.SemaphoreType.DMA((pieces,)),
            pltpu.SemaphoreType.DMA((tp_size,)),
            pltpu.SemaphoreType.DMA((tp_size,)),
        ],
        compiler_params=pltpu.CompilerParams(
            collective_id=place_id, has_side_effects=True, vmem_limit_bytes=56 * 1024 * 1024
        ),
        cost_estimate=pl.CostEstimate(
            flops=40 * slots * width, bytes_accessed=6 * slots * width, transcendentals=0
        ),
    )(jnp.broadcast_to(ids[:, None], (slots, LANES)), places, ref_logits, pol_logits)


def shards(ref_logits, token_ids, old_logp, owner_of_row, lengths, rewards, group_ids, pol_logits):
    role_count = lax.axis_size("role")
    data_count = lax.axis_size("dp")
    owner_count = role_count * data_count
    my_owner = lax.axis_index("role") * data_count + lax.axis_index("dp")
    row_count = ref_logits.shape[0]
    vocab_local = ref_logits.shape[1]
    slot_count = pol_logits.shape[0]
    capacity = slot_count // owner_count
    seq_count = rewards.shape[0]
    seq_local = lengths.shape[0]
    row_span = row_count // seq_local
    member = group_ids[:, None] == group_ids[None, :]
    group_total = jnp.sum(jnp.where(member, rewards[None, :], 0.0), axis=1)
    group_count = jnp.sum(member.astype(jnp.float32), axis=1)
    advantage = rewards - group_total / jnp.maximum(group_count, 1.0)

    row_index = jnp.arange(row_count)
    row_valid = row_index % row_span < jnp.repeat(lengths, row_span)
    tag = owner_of_row * 2 + row_valid.astype(jnp.int32)
    local = jnp.stack([part.astype(jnp.float32) for part in (tag, token_ids, old_logp)])
    every = lax.all_gather(local, ("role", "dp"), axis=0, tiled=False)
    every_tag = every[:, 0].astype(jnp.int32)
    every_owner = every_tag // 2
    every_valid = every_tag % 2
    every_ids = every[:, 1].astype(jnp.int32)
    every_old = every[:, 2]
    valid_total = jnp.sum(every_valid).astype(jnp.float32)
    before = row_index[None, :] < row_index[:, None]
    mine = every_owner == my_owner
    my_rank = jnp.sum((mine[:, None, :] & before[None]).astype(jnp.int32), axis=2)
    slot_pos = jnp.arange(capacity)
    match = mine[:, None, :] & (my_rank[:, None, :] == slot_pos[None, :, None])
    take = lambda values: jnp.sum(jnp.where(match, values[:, None, :], 0), axis=2).reshape(slot_count)
    got_ids = take(every_ids)
    got_old = take(every_old)
    slot_valid = take(every_valid) > 0
    every_adv = jnp.repeat(advantage.reshape(owner_count, seq_local), row_span, axis=1)
    slot_adv = take(every_adv)
    near_ids = got_ids - lax.axis_index("tp") * vocab_local

    if role_count == 4 and data_count == 2 and vocab_local % (2 * LANES) == 0:
        places, need, _ = hop_places(
            every_owner.reshape(-1), every_valid.reshape(-1) > 0, my_owner, capacity, row_count
        )
        level = jnp.int32(0)
        for caps in CLASSES[:-1]:
            fits = [count <= cap for count, cap in zip(need, caps)]
            level = level + 1 - (fits[0] & fits[1] & fits[2]).astype(jnp.int32)
        branches = [
            functools.partial(route, caps, 1 + place) for place, caps in enumerate(CLASSES)
        ]
        got_rows, stats = lax.switch(
            level, branches, places, near_ids, ref_logits, pol_logits
        )
        stats = stats[:, :6, :slot_count]
    else:
        same = owner_of_row[:, None] == owner_of_row[None, :]
        rank = jnp.sum((same & before).astype(jnp.int32), axis=1)
        got_rows = fetch_rows(ref_logits, rank, owner_of_row, owner_count, capacity)
        stats = row_call(
            stats_kernel, LANES, jnp.float32, 20, near_ids, (), (pol_logits, got_rows)
        )[:, :6]
        stats = lax.all_gather(stats.T, "tp", axis=0, tiled=False)
    near_p, near_q = stats[:, 0], stats[:, 1]
    peak_p = jnp.max(near_p, axis=0)
    peak_q = jnp.max(near_q, axis=0)
    shift_p = jnp.exp(near_p - peak_p)
    shift_q = jnp.exp(near_q - peak_q)
    total_p = jnp.sum(stats[:, 2] * shift_p, axis=0)
    cross_sum = jnp.sum(stats[:, 3] * shift_p, axis=0)
    token_logit = jnp.sum(stats[:, 4], axis=0)
    total_q = jnp.sum(stats[:, 5] * shift_q, axis=0)

    loss_scale = row_count * owner_count / valid_total
    log_p = peak_p + jnp.log(total_p)
    log_q = peak_q + jnp.log(total_q)
    mean_gap = cross_sum / total_p
    kl_term = mean_gap - log_p + log_q
    raw_log_ratio = token_logit - log_p - got_old
    prob_ratio = jnp.exp(jnp.clip(raw_log_ratio, -ratio_clamp, ratio_clamp))
    plain_loss = -slot_adv * prob_ratio
    clipped_loss = -slot_adv * jnp.clip(prob_ratio, low_bound, high_bound)
    upper_loss = jnp.maximum(plain_loss, clipped_loss)
    dual_loss = -dual_bound * slot_adv
    negative = slot_adv < 0.0
    policy_loss = jnp.where(negative, jnp.minimum(upper_loss, dual_loss), upper_loss)
    token_losses = jnp.where(slot_valid, policy_loss + kl_weight * kl_term, 0.0)
    inside = (prob_ratio > low_bound) & (prob_ratio < high_bound)
    token_coef = jnp.where((plain_loss >= clipped_loss) | inside, plain_loss, 0.0)
    token_coef = jnp.where(negative & (upper_loss > dual_loss), 0.0, token_coef)
    token_coef = jnp.where(jnp.abs(raw_log_ratio) < ratio_clamp, token_coef, 0.0)
    scale = jnp.where(slot_valid, loss_scale, 0.0)
    slope = scale * kl_weight / total_p
    base = -scale * (token_coef + kl_weight * mean_gap) / total_p
    bump = scale * token_coef
    per_row = jnp.stack([peak_p, slope, base, bump], axis=1)
    per_row = jnp.pad(per_row, ((0, 0), (0, LANES - 4)))
    grad_rows = row_call(
        grad_kernel, vocab_local, jnp.bfloat16, 10, near_ids, (per_row,), (pol_logits, got_rows)
    )
    return (grad_rows, token_losses)


def solution(mesh):
    return jax.shard_map(
        shards,
        mesh=mesh,
        in_specs=(
            P(("role", "dp"), "tp"),
            P(("role", "dp")),
            P(("role", "dp")),
            P(("role", "dp")),
            P(("role", "dp")),
            P(),
            P(),
            P(("role", "dp"), "tp"),
        ),
        out_specs=(P(("role", "dp"), "tp"), P(("role", "dp"))),
        check_vma=False,
    )
```
